32 devices in a mesh: parts: 2 (over y), seq: 4 (over z), head: 4 (over x, core).
Axes of the slice: x: 2, y: 2, z: 4, core: 2. Of those that a mesh axis runs over, the one named last changes fastest.
Arguments:
- query_rows: bfloat16 [6144, 4096], P(('parts', 'seq', 'head')), parts along dimension 0, may hold values from -12 to 12
- key_rows: bfloat16 [6144, 4096], P(('parts', 'seq', 'head')), parts along dimension 0, may hold values from -12 to 12
- value_rows: bfloat16 [6144, 4096], P(('parts', 'seq', 'head')), parts along dimension 0, may hold values from -6 to 6
- block_lists: int32 [64, 4, 4, 3], P('parts', 'seq'), parts along dimension 0, may hold values from 0 to 5, as said below
- block_counts: int32 [64, 4, 4], P('parts'), parts along dimension 0, may hold values from 0 to 3, as said below
Outputs:
- attended: bfloat16 [6144, 4096], P(('parts', 'seq', 'head')), parts along dimension 0
The draws below stay inside these ranges and needn't reach their ends.
There are 2 independent parts, one for each index of `parts`. The reference program is written for one: setup_inputs(seed, part) draws one part's arguments, and reference() takes and returns one part's arrays. A program takes and returns all parts, laid end to end along the dimension named above; each array names one. Nothing has to cross between parts.
Inputs may be any that keep to these rules, and one draw needn't show every extreme that they name: `block_lists`: for one head, query tile and key tile the 3 entries are distinct block numbers of the key tile; only the first block_counts of them are listed. `block_counts`: 0 where the key tile is the query tile; some entries of every draw equal 3; for every k, query tile and key tile, the counts of heads 2k and 2k+1 sum to at most 4, and exactly 4 for some k in every draw.
All inputs are finite; a program needn't handle non-finite values.
Results may differ from the reference program's by a relative error of at most 0.0034.
Values may be sent and summed in bfloat16 or wider, within the bound.
No kernel may reach another device: no remote copies, remote signals or barrier semaphores. Data moves between devices by JAX's collectives and lax.ppermute only.
A program may use at most 64 MiB of HBM per device.

```python
import math
import jax
import jax.numpy as jnp
from jax import lax

HEADS = 32
DH = 128
BLOCK = 128
MOST = 3
PAIR_MOST = 4
TILE = 768
TILES = 4
SEQ_LEN = 3072


def draw_query_rows(key, part):
    bulk = jnp.clip(1.75 * jax.random.normal(jax.random.fold_in(key, 41), (SEQ_LEN, HEADS * DH), jnp.float32), -12.0, 12.0)
    return bulk.astype(jnp.bfloat16)


def draw_key_rows(key, part):
    bulk = jnp.clip(1.75 * jax.random.normal(jax.random.fold_in(key, 43), (SEQ_LEN, HEADS * DH), jnp.float32), -12.0, 12.0)
    return bulk.astype(jnp.bfloat16)


def draw_block_lists(key, part):
    block_total = TILE // BLOCK
    scores = jax.random.randint(jax.random.fold_in(key, 21), (HEADS, TILES, TILES, block_total), 0, 1 << 20)
    scores = scores * block_total + jnp.arange(block_total, dtype=jnp.int32)
    return lax.top_k(scores, MOST)[1].astype(jnp.int32)


def draw_block_counts(key, part):
    pair_total = HEADS // 2
    density_level = jax.random.permutation(jax.random.fold_in(key, 31), pair_total) % 3
    busy_sum = jax.random.randint(jax.random.fold_in(key, 32), (pair_total, TILES, TILES), MOST, PAIR_MOST + 1)
    sparse_sum = jax.random.randint(jax.random.fold_in(key, 33), (pair_total, TILES, TILES), 0, 2)
    level_grid = density_level[:, None, None]
    pair_sum = jnp.where(level_grid == 2, PAIR_MOST, jnp.where(level_grid == 1, busy_sum, sparse_sum))
    lower_end = jnp.maximum(pair_sum - MOST, 0)
    upper_end = jnp.minimum(pair_sum, MOST)
    split_draw = jax.random.randint(jax.random.fold_in(key, 34), (pair_total, TILES, TILES), 0, 1 << 20)
    first_count = lower_end + split_draw % (upper_end - lower_end + 1)
    first_count = jnp.where(level_grid == 2, MOST, first_count)
    second_count = pair_sum - first_count
    counts_grid = jnp.stack([first_count, second_count], axis=1).reshape(HEADS, TILES, TILES)
    own_tile = jnp.arange(TILES)[:, None] == jnp.arange(TILES)[None, :]
    return jnp.where(own_tile[None], 0, counts_grid).astype(jnp.int32)


def steps_of(key, dims, split, least, high):
    level, own = 1.0, jax.random.fold_in(key, 6)
    for position, blocks in split:
        heights = jnp.exp(jax.random.uniform(jax.random.fold_in(own, position), (blocks,), jnp.float32, least / len(split), high / len(split)))
        level = level * jnp.repeat(heights, dims[position] // blocks).reshape([-1 if axis == position else 1 for axis in range(len(dims))])
    return level


def centred(stream_key, extent, deviation, bound, split=(), held_as=jnp.bfloat16):
    factor_of = steps_of(stream_key, extent, split, -0.22, 0.18) if split else 1.0
    values = jax.random.normal(stream_key, extent, jnp.float32) * deviation * factor_of
    return jnp.minimum(jnp.maximum(values, -bound), bound).astype(held_as)


def setup_inputs(seed: int = 0, part: int = 0) -> dict:
    seeds = jax.random.split(jax.random.key(seed), 6)
    part_splits = jax.random.split(jax.random.fold_in(seeds[5], part), 6)
    query_rows = draw_query_rows(jax.random.fold_in(jax.random.fold_in(seeds[5], part), 71), part)
    key_rows = draw_key_rows(jax.random.fold_in(jax.random.fold_in(seeds[5], part), 71), part)
    value_rows = centred(part_splits[2], (SEQ_LEN, HEADS * DH), 1.0, 6.0, ((0, 16),))
    block_lists = draw_block_lists(jax.random.fold_in(jax.random.fold_in(seeds[5], part), 71), part)
    block_counts = draw_block_counts(jax.random.fold_in(jax.random.fold_in(seeds[5], part), 71), part)
    return dict(query_rows=query_rows, key_rows=key_rows, value_rows=value_rows, block_lists=block_lists, block_counts=block_counts)


def reference(query_rows, key_rows, value_rows, block_lists, block_counts):
    block_total = TILE // BLOCK
    score_scale = 1.0 / math.sqrt(DH)

    def one_head(head_index):
        head_queries = lax.dynamic_slice_in_dim(query_rows, head_index * DH, DH, 1)
        head_keys = lax.dynamic_slice_in_dim(key_rows, head_index * DH, DH, 1)
        head_values = lax.dynamic_slice_in_dim(value_rows, head_index * DH, DH, 1)
        key_blocks = head_keys.reshape(TILES * block_total, BLOCK, DH)
        value_blocks = head_values.reshape(TILES * block_total, BLOCK, DH)

        def one_tile(tile_index):
            tile_queries = lax.dynamic_slice_in_dim(head_queries, tile_index * TILE, TILE, 0)
            own_keys = lax.dynamic_slice_in_dim(head_keys, tile_index * TILE, TILE, 0)
            own_values = lax.dynamic_slice_in_dim(head_values, tile_index * TILE, TILE, 0)
            tile_lists = block_lists[head_index, tile_index].astype(jnp.int32)
            tile_counts = block_counts[head_index, tile_index].astype(jnp.int32)
            picks = (jnp.arange(TILES, dtype=jnp.int32)[:, None] * block_total + tile_lists).reshape(-1)
            live_slots = (jnp.arange(MOST, dtype=jnp.int32)[None, :] < tile_counts[:, None]).reshape(-1)
            far_keys = key_blocks[picks].reshape(TILES * MOST * BLOCK, DH)
            far_values = value_blocks[picks].reshape(TILES * MOST * BLOCK, DH)
            all_keys = jnp.concatenate([own_keys, far_keys], axis=0)
            all_values = jnp.concatenate([own_values, far_values], axis=0)
            live_keys = jnp.concatenate([jnp.ones((TILE,), bool), jnp.repeat(live_slots, BLOCK)])
            scores = jnp.dot(tile_queries, all_keys.T, preferred_element_type=jnp.float32) * score_scale
            scores = jnp.where(live_keys[None, :], scores, -jnp.inf)
            row_top = lax.optimization_barrier(jnp.max(scores, axis=1, keepdims=True))
            weights = jnp.exp(scores - row_top)
            denominator = lax.optimization_barrier(jnp.sum(weights, axis=1, keepdims=True))
            mixture = jnp.dot(weights.astype(jnp.bfloat16), all_values, preferred_element_type=jnp.float32)
            return (mixture / denominator).astype(jnp.bfloat16)
        return lax.map(one_tile, jnp.arange(TILES, dtype=jnp.int32))
    head_outputs = lax.map(one_head, jnp.arange(HEADS, dtype=jnp.int32))
    head_outputs = head_outputs.reshape(HEADS, TILES * TILE, DH)
    return jnp.transpose(head_outputs, (1, 0, 2)).reshape(TILES * TILE, HEADS * DH)
```

```python
import functools
import math

import jax
import jax.numpy as jnp
from jax import lax
from jax.experimental import pallas as pl
from jax.experimental.pallas import tpu as pltpu
from jax.sharding import PartitionSpec as P

HEADS = 32
DH = 128
BLOCK = 128
MOST = 3
PAIR_MOST = 4
TILE = 768
PAIR = 2 * DH
OWN_BLOCKS = TILE // BLOCK
VMEM_LIMIT = 32 * 1024 * 1024
SMEM = pltpu.SMEM


def shifted(array, axis, step):
    size = lax.axis_size(axis)
    return lax.ppermute(array, axis, [(i, (i + step) % size) for i in range(size)])


def vmem_spec():
    return pl.BlockSpec(memory_space=pltpu.VMEM)


def smem_spec():
    return pl.BlockSpec(memory_space=SMEM)


def pick_kernel(head_count, seq_count, slots, place_ref, counts_ref, *refs):
    want_refs = refs[: seq_count - 1]
    rows_refs = refs[seq_count - 1 : seq_count - 1 + head_count]
    tile_ref = refs[seq_count - 1 + head_count]
    send_refs = refs[seq_count + head_count :]
    my_seq, my_head = place_ref[0], place_ref[1]
    rows = TILE // head_count
    for step in range(head_count):
        rank = lax.rem(my_head - step + head_count, head_count)
        place = pl.ds(pl.multiple_of(rank * rows, 16), rows)
        for pair in range(slots):
            for half in range(2):
                base = pair * 2 * PAIR + half * DH
                tile_ref[2 * pair + half, place, :DH] = rows_refs[step][:, base : base + DH]
                tile_ref[2 * pair + half, place, DH:] = rows_refs[step][
                    :, base + PAIR : base + PAIR + DH
                ]
    for step in range(1, seq_count):
        asker = lax.rem(my_seq + step, seq_count)
        for pair in range(slots):
            first = 2 * place_ref[2 + pair]
            first_count = counts_ref[(first * seq_count + asker) * seq_count + my_seq]
            both = first_count + counts_ref[((first + 1) * seq_count + asker) * seq_count + my_seq]
            for slot in range(PAIR_MOST):

                @pl.when(slot < both)
                def _():
                    half = jnp.where(slot < first_count, 0, 1)
                    entry = jnp.where(slot < first_count, slot, slot - first_count)
                    entry = jnp.clip(entry, 0, MOST - 1)
                    block = want_refs[step - 1][
                        ((first + half) * seq_count + my_seq) * MOST + entry
                    ]
                    send_refs[step - 1][pair * PAIR_MOST + slot] = tile_ref[
                        2 * pair + half, pl.ds(pl.multiple_of(block * BLOCK, BLOCK), BLOCK), :
                    ]


def pick_blocks(places, counts, wanted, pieces, slots):
    head_count, seq_count = len(pieces), len(wanted) + 1
    out_shape = [jax.ShapeDtypeStruct((2 * slots, TILE, 2 * DH), jnp.bfloat16)]
    out_shape += [
        jax.ShapeDtypeStruct((slots * PAIR_MOST, BLOCK, 2 * DH), jnp.bfloat16)
    ] * (seq_count - 1)
    outs = pl.pallas_call(
        functools.partial(pick_kernel, head_count, seq_count, slots),
        out_shape=out_shape,
        in_specs=[smem_spec()] * (seq_count + 1) + [vmem_spec()] * head_count,
        out_specs=[vmem_spec()] * seq_count,
        compiler_params=pltpu.CompilerParams(vmem_limit_bytes=VMEM_LIMIT),
        cost_estimate=pl.CostEstimate(
            flops=0, bytes_accessed=slots * 5 * 1024 * 1024, transcendentals=0
        ),
        name="pick_blocks",
    )(places, counts, *wanted, *pieces)
    return outs[0], outs[1:]


GROUP = 3 * BLOCK
QUERIES = 256


def fold(values, combine):
    total = values[:, :DH]
    for start in range(DH, values.shape[1], DH):
        total = combine(total, values[:, start : start + DH])
    return total


def row_top(scores):
    top = jnp.max(fold(scores, jnp.maximum), axis=1, keepdims=True)
    return jnp.broadcast_to(top, (scores.shape[0], DH))


def weigh(scores, top):
    return jnp.concatenate(
        [jnp.exp2(scores[:, at : at + DH] - top) for at in range(0, scores.shape[1], DH)], axis=1
    )


def attend_kernel(head_count, seq_count, place_ref, counts_ref, tile_ref, *refs):
    query_refs = refs[:head_count]
    block_refs = refs[head_count : head_count + seq_count - 1]
    out_refs = refs[head_count + seq_count - 1 : 2 * head_count + seq_count - 1]
    q_ref, k_ref, v_ref, top_ref, sum_ref, mix_ref = refs[2 * head_count + seq_count - 1 :]
    my_seq = place_ref[0]
    turn = pl.program_id(0)
    half = lax.rem(turn, 2)
    first = 2 * place_ref[2 + turn // 2]
    rows = TILE // head_count
    scale = math.log2(math.e) / math.sqrt(DH)

    @pl.when(turn == 0)
    def _():
        k_ref[...] = jnp.zeros_like(k_ref)
        v_ref[...] = jnp.zeros_like(v_ref)

    for step in range(head_count):
        q_ref[step * rows : (step + 1) * rows, :] = query_refs[step][...]

    used = jnp.int32(0)
    for step in range(1, seq_count):
        holder = lax.rem(my_seq - step + seq_count, seq_count)
        first_count = counts_ref[(first * seq_count + my_seq) * seq_count + holder]
        second_count = counts_ref[((first + 1) * seq_count + my_seq) * seq_count + holder]
        count = jnp.where(half == 0, first_count, second_count)
        start = jnp.where(half == 0, 0, first_count)
        for entry in range(MOST):

            @pl.when(entry < count)
            def _():
                place = pl.ds(pl.multiple_of((used + entry) * BLOCK, BLOCK), BLOCK)
                slot = jnp.minimum(start + entry, PAIR_MOST - 1)
                k_ref[place, :] = block_refs[step - 1][slot, :, :DH]
                v_ref[place, :] = block_refs[step - 1][slot, :, DH:]

        used = used + count

    def score(queries, keys):
        return (
            lax.dot_general(
                queries, keys, (((1,), (1,)), ((), ())), preferred_element_type=jnp.float32
            )
            * scale
        )

    own_keys = tile_ref[0, :, :DH]
    own_values = tile_ref[0, :, DH:]
    for at in range(0, TILE, QUERIES):
        span = slice(at, at + QUERIES)
        scores = score(q_ref[span, :], own_keys)
        top = row_top(scores)
        weights = weigh(scores, top)
        top_ref[span, :] = top
        sum_ref[span, :] = fold(weights, jnp.add)
        mix_ref[span, :] = jnp.dot(
            weights.astype(jnp.bfloat16), own_values, preferred_element_type=jnp.float32
        )

    def visit(group, carry):
        place = pl.ds(pl.multiple_of(group * GROUP, GROUP), GROUP)
        keys = k_ref[place, :]
        values = v_ref[place, :]
        column = lax.broadcasted_iota(jnp.int32, (1, GROUP), 1) + group * GROUP
        bias = jnp.where(column < used * BLOCK, 0.0, -jnp.inf)
        for at in range(0, TILE, QUERIES):
            span = slice(at, at + QUERIES)
            scores = score(q_ref[span, :], keys) + bias
            old_top = top_ref[span, :]
            top = jnp.maximum(old_top, row_top(scores))
            weights = weigh(scores, top)
            rescale = jnp.exp2(old_top - top)
            top_ref[span, :] = top
            sum_ref[span, :] = sum_ref[span, :] * rescale + fold(weights, jnp.add)
            mix_ref[span, :] = mix_ref[span, :] * rescale + jnp.dot(
                weights.astype(jnp.bfloat16), values, preferred_element_type=jnp.float32
            )
        return carry

    lax.fori_loop(0, (used + 2) // 3, visit, 0)
    for step in range(head_count):
        span = slice(step * rows, (step + 1) * rows)
        total = jnp.sum(sum_ref[span, :], axis=1, keepdims=True)
        out_refs[step][...] = (mix_ref[span, :] / total).astype(jnp.bfloat16)


def attend(places, counts, tile_pairs, queries, blocks, first_pair, slots):
    head_count, seq_count = len(queries), len(blocks) + 1
    rows = TILE // head_count
    most_blocks = -(-(seq_count - 1) * MOST // 3) * 3
    return pl.pallas_call(
        functools.partial(attend_kernel, head_count, seq_count),
        grid=(2 * slots,),
        out_shape=[jax.ShapeDtypeStruct((rows, slots * PAIR), jnp.bfloat16)] * head_count,
        in_specs=[smem_spec()] * 2
        + [pl.BlockSpec((1, TILE, 2 * DH), lambda i: (i, 0, 0))]
        + [pl.BlockSpec((rows, DH), lambda i: (0, 2 * first_pair + i))] * head_count
        + [pl.BlockSpec((PAIR_MOST, BLOCK, 2 * DH), lambda i: (i // 2, 0, 0))] * (seq_count - 1),
        out_specs=[pl.BlockSpec((rows, DH), lambda i: (0, i))] * head_count,
        scratch_shapes=[
            pltpu.VMEM((TILE, DH), jnp.bfloat16),
            pltpu.VMEM((most_blocks * BLOCK, DH), jnp.bfloat16),
            pltpu.VMEM((most_blocks * BLOCK, DH), jnp.bfloat16),
            pltpu.VMEM((TILE, DH), jnp.float32),
            pltpu.VMEM((TILE, DH), jnp.float32),
            pltpu.VMEM((TILE, DH), jnp.float32),
        ],
        compiler_params=pltpu.CompilerParams(vmem_limit_bytes=VMEM_LIMIT),
        cost_estimate=pl.CostEstimate(
            flops=slots * 2 * TILE * 2 * TILE * DH * 4,
            bytes_accessed=slots * 3 * 1024 * 1024,
            transcendentals=slots * 2 * TILE * 2 * TILE,
        ),
        name="attend",
    )(places, counts, tile_pairs, *queries, *blocks)


def lay_kernel(head_count, groups, place_ref, *refs):
    piece_refs = refs[: head_count * len(groups)]
    out_ref = refs[head_count * len(groups)]
    sems = refs[head_count * len(groups) + 1]
    my_head = place_ref[0]
    local_pairs = sum(len(group) for group in groups)
    copies = []
    for number, group in enumerate(groups):
        for step in range(head_count):
            rank = lax.rem(my_head - step + head_count, head_count)
            for at, pair in enumerate(group):
                column = place_ref[1 + rank * local_pairs + pair] * PAIR
                copy = pltpu.make_async_copy(
                    piece_refs[number * head_count + step].at[:, at * PAIR : (at + 1) * PAIR],
                    out_ref.at[:, pl.ds(pl.multiple_of(column, PAIR), PAIR)],
                    sems.at[len(copies)],
                )
                copy.start()
                copies.append(copy)
    for copy in copies:
        copy.wait()


def lay_out(places, pieces, groups, rows):
    head_count = len(pieces[0])
    flat = [piece for stage in pieces for piece in stage]
    copies = head_count * sum(len(group) for group in groups)
    return pl.pallas_call(
        functools.partial(lay_kernel, head_count, groups),
        out_shape=jax.ShapeDtypeStruct((rows, HEADS * DH), jnp.bfloat16),
        in_specs=[smem_spec()] + [pl.BlockSpec(memory_space=pl.ANY)] * len(flat),
        out_specs=pl.BlockSpec(memory_space=pl.ANY),
        scratch_shapes=[pltpu.SemaphoreType.DMA((copies,))],
        name="lay_out",
    )(places, *flat)


def on_device(query_rows, key_rows, value_rows, block_lists, block_counts):
    head_count = lax.axis_size("head")
    seq_count = lax.axis_size("seq")
    seq_rank = lax.axis_index("seq")
    head_rank = lax.axis_index("head")
    rows = query_rows.shape[0]
    local_pairs = HEADS // 2 // head_count
    pair_table = jnp.arange(HEADS // 2, dtype=jnp.int32)
    groups = [[0], list(range(1, local_pairs - 1)), [local_pairs - 1]]
    groups = [group for group in groups if group] if local_pairs > 1 else [[0]]

    lists = block_lists.reshape(-1)
    counts = block_counts.reshape(-1)
    wanted = [shifted(lists, "seq", (seq_count - step) % seq_count) for step in range(1, seq_count)]

    def columns(array, rank, pair):
        at = lax.dynamic_slice_in_dim(pair_table, rank * local_pairs + pair, 1)[0] * PAIR
        return lax.dynamic_slice(array, (0, at), (rows, PAIR))

    def gathered(parts):
        pieces = []
        for step in range(head_count):
            rank = (head_rank + step) % head_count
            piece = jnp.concatenate([columns(array, rank, pair) for array, pair in parts], axis=1)
            pieces.append(piece if step == 0 else shifted(piece, "head", step))
        return pieces

    tiles, sends = [], []
    for number, group in enumerate(groups):
        parts = [(array, pair) for pair in group for array in (key_rows, value_rows)]
        pieces = gathered(parts)
        mine = lax.dynamic_slice_in_dim(pair_table, head_rank * local_pairs + group[0], len(group))
        places = jnp.concatenate([jnp.stack([seq_rank, head_rank]).astype(jnp.int32), mine])
        tile_pairs, picked = pick_blocks(places, counts, wanted, pieces, len(group))
        blocks = [shifted(picked[step - 1], "seq", step) for step in range(1, seq_count)]
        tiles.append((places, tile_pairs, blocks))
    queries = gathered([(query_rows, pair) for pair in range(local_pairs)])

    results = []
    for group, (places, tile_pairs, blocks) in zip(groups, tiles):
        outs = attend(places, counts, tile_pairs, queries, blocks, group[0], len(group))
        results.append(
            [outs[0]]
            + [shifted(outs[head_count - step], "head", step) for step in range(1, head_count)]
        )
    places = jnp.concatenate([head_rank.astype(jnp.int32)[None], pair_table])
    return lay_out(places, results, groups, rows)


def solution(mesh):
    in_specs = (
        P(("parts", "seq", "head"), None),
        P(("parts", "seq", "head"), None),
        P(("parts", "seq", "head"), None),
        P("parts", "seq", None, None),
        P("parts", None, None),
    )
    out_specs = P(("parts", "seq", "head"), None)
    return jax.shard_map(
        on_device, mesh=mesh, in_specs=in_specs, out_specs=out_specs, check_vma=False
    )
```

```python
import functools
import math

import jax
import jax.numpy as jnp
from jax import lax
from jax.experimental import pallas as pl
from jax.experimental.pallas import tpu as pltpu
from jax.sharding import PartitionSpec as P

HEADS = 32
DH = 128
BLOCK = 128
MOST = 3
PAIR_MOST = 4
TILE = 768
PAIR = 2 * DH
OWN_BLOCKS = TILE // BLOCK
VMEM_LIMIT = 32 * 1024 * 1024
SMEM = pltpu.SMEM


def shifted(array, axis, step):
    size = lax.axis_size(axis)
    return lax.ppermute(array, axis, [(i, (i + step) % size) for i in range(size)])


def vmem_spec():
    return pl.BlockSpec(memory_space=pltpu.VMEM)


def smem_spec():
    return pl.BlockSpec(memory_space=SMEM)


def gather_kernel(table_ref, *refs):
    out_ref = refs[-1]
    for at, ref in enumerate(refs[:-1]):
        out_ref[0, :, at * PAIR : (at + 1) * PAIR] = ref[...]


def gather_columns(table, parts, head_count, local_pairs):
    rows = parts[0][0].shape[0]

    def column_of(pair):
        return lambda rank, table_ref: (0, table_ref[rank * local_pairs + pair])

    return pl.pallas_call(
        gather_kernel,
        grid_spec=pltpu.PrefetchScalarGridSpec(
            num_scalar_prefetch=1,
            grid=(head_count,),
            in_specs=[pl.BlockSpec((rows, PAIR), column_of(pair)) for _, pair in parts],
            out_specs=pl.BlockSpec((1, rows, len(parts) * PAIR), lambda rank, _: (rank, 0, 0)),
        ),
        out_shape=jax.ShapeDtypeStruct((head_count, rows, len(parts) * PAIR), jnp.bfloat16),
        compiler_params=pltpu.CompilerParams(vmem_limit_bytes=VMEM_LIMIT),
        cost_estimate=pl.CostEstimate(
            flops=0, bytes_accessed=len(parts) * TILE * PAIR * 4, transcendentals=0
        ),
        name="gather_columns",
    )(table, *[array for array, _ in parts])


def pick_kernel(seq_count, slots, place_ref, counts_ref, *refs):
    want_refs = refs[: seq_count - 1]
    tile_ref = refs[seq_count - 1]
    send_refs = refs[seq_count:]
    my_seq = place_ref[0]
    for step in range(1, seq_count):
        asker = lax.rem(my_seq + step, seq_count)
        for pair in range(slots):
            first = 2 * place_ref[2 + pair]
            first_count = counts_ref[(first * seq_count + asker) * seq_count + my_seq]
            both = first_count + counts_ref[((first + 1) * seq_count + asker) * seq_count + my_seq]
            for slot in range(PAIR_MOST):

                @pl.when(slot < both)
                def _():
                    half = jnp.where(slot < first_count, 0, 1)
                    entry = jnp.where(slot < first_count, slot, slot - first_count)
                    entry = jnp.clip(entry, 0, MOST - 1)
                    block = want_refs[step - 1][
                        ((first + half) * seq_count + my_seq) * MOST + entry
                    ]
                    span = pl.ds(pl.multiple_of(block * BLOCK, BLOCK), BLOCK)
                    base = pair * 2 * PAIR + half * DH
                    where = pair * PAIR_MOST + slot
                    send_refs[step - 1][where, :, :DH] = tile_ref[
                        span, pl.ds(pl.multiple_of(base, DH), DH)
                    ]
                    send_refs[step - 1][where, :, DH:] = tile_ref[
                        span, pl.ds(pl.multiple_of(base + PAIR, DH), DH)
                    ]


def pick_blocks(places, counts, wanted, tile, slots):
    seq_count = len(wanted) + 1
    return pl.pallas_call(
        functools.partial(pick_kernel, seq_count, slots),
        grid=(1,),
        out_shape=[jax.ShapeDtypeStruct((slots * PAIR_MOST, BLOCK, 2 * DH), jnp.bfloat16)]
        * (seq_count - 1),
        in_specs=[smem_spec()] * (seq_count + 1)
        + [pl.BlockSpec((TILE, slots * 2 * PAIR), lambda i: (0, 0))],
        out_specs=[pl.BlockSpec((slots * PAIR_MOST, BLOCK, 2 * DH), lambda i: (0, 0, 0))]
        * (seq_count - 1),
        compiler_params=pltpu.CompilerParams(vmem_limit_bytes=VMEM_LIMIT),
        cost_estimate=pl.CostEstimate(
            flops=0, bytes_accessed=slots * 2 * 1024 * 1024, transcendentals=0
        ),
        name="pick_blocks",
    )(places, counts, *wanted, tile)


GROUP = 3 * BLOCK
QUERIES = 256


def fold(values, combine):
    total = values[:, :DH]
    for start in range(DH, values.shape[1], DH):
        total = combine(total, values[:, start : start + DH])
    return total


def row_top(scores):
    top = jnp.max(fold(scores, jnp.maximum), axis=1, keepdims=True)
    return jnp.broadcast_to(top, (scores.shape[0], DH))


def weigh(scores, top):
    return jnp.concatenate(
        [jnp.exp2(scores[:, at : at + DH] - top) for at in range(0, scores.shape[1], DH)], axis=1
    )


def attend_kernel(seq_count, place_ref, counts_ref, q_ref, own_k_ref, own_v_ref, *refs):
    block_refs = refs[: seq_count - 1]
    out_ref, k_ref, v_ref, top_ref, sum_ref, mix_ref = refs[seq_count - 1 :]
    my_seq = place_ref[0]
    turn = pl.program_id(0)
    half = lax.rem(turn, 2)
    first = 2 * place_ref[2 + turn // 2]
    scale = math.log2(math.e) / math.sqrt(DH)

    @pl.when(turn == 0)
    def _():
        k_ref[...] = jnp.zeros_like(k_ref)
        v_ref[...] = jnp.zeros_like(v_ref)

    used = jnp.int32(0)
    for step in range(1, seq_count):
        holder = lax.rem(my_seq - step + seq_count, seq_count)
        first_count = counts_ref[(first * seq_count + my_seq) * seq_count + holder]
        second_count = counts_ref[((first + 1) * seq_count + my_seq) * seq_count + holder]
        count = jnp.where(half == 0, first_count, second_count)
        start = jnp.where(half == 0, 0, first_count)
        for entry in range(MOST):

            @pl.when(entry < count)
            def _():
                place = pl.ds(pl.multiple_of((used + entry) * BLOCK, BLOCK), BLOCK)
                slot = jnp.minimum(start + entry, PAIR_MOST - 1)
                k_ref[place, :] = block_refs[step - 1][slot, :, :DH]
                v_ref[place, :] = block_refs[step - 1][slot, :, DH:]

        used = used + count

    def score(queries, keys):
        return (
            lax.dot_general(
                queries, keys, (((1,), (1,)), ((), ())), preferred_element_type=jnp.float32
            )
            * scale
        )

    own_keys = own_k_ref[...]
    own_values = own_v_ref[...]
    for at in range(0, TILE, QUERIES):
        span = slice(at, at + QUERIES)
        scores = score(q_ref[span, :], own_keys)
        top = row_top(scores)
        weights = weigh(scores, top)
        top_ref[span, :] = top
        sum_ref[span, :] = fold(weights, jnp.add)
        mix_ref[span, :] = jnp.dot(
            weights.astype(jnp.bfloat16), own_values, preferred_element_type=jnp.float32
        )

    def visit(group, carry):
        place = pl.ds(pl.multiple_of(group * GROUP, GROUP), GROUP)
        keys = k_ref[place, :]
        values = v_ref[place, :]
        column = lax.broadcasted_iota(jnp.int32, (1, GROUP), 1) + group * GROUP
        bias = jnp.where(column < used * BLOCK, 0.0, -jnp.inf)
        for at in range(0, TILE, QUERIES):
            span = slice(at, at + QUERIES)
            scores = score(q_ref[span, :], keys) + bias
            old_top = top_ref[span, :]
            top = jnp.maximum(old_top, row_top(scores))
            weights = weigh(scores, top)
            rescale = jnp.exp2(old_top - top)
            top_ref[span, :] = top
            sum_ref[span, :] = sum_ref[span, :] * rescale + fold(weights, jnp.add)
            mix_ref[span, :] = mix_ref[span, :] * rescale + jnp.dot(
                weights.astype(jnp.bfloat16), values, preferred_element_type=jnp.float32
            )
        return carry

    lax.fori_loop(0, (used + 2) // 3, visit, 0)
    for at in range(0, TILE, QUERIES):
        span = slice(at, at + QUERIES)
        total = jnp.sum(sum_ref[span, :], axis=1, keepdims=True)
        out_ref[span, :] = (mix_ref[span, :] / total).astype(jnp.bfloat16)


def attend(places, counts, queries, query_at, tile, blocks, slots):
    seq_count = len(blocks) + 1
    most_blocks = -(-(seq_count - 1) * MOST // 3) * 3

    def head_block(index):
        return pl.BlockSpec((TILE, DH), lambda i: (0, index(i)))

    return pl.pallas_call(
        functools.partial(attend_kernel, seq_count),
        grid=(2 * slots,),
        out_shape=jax.ShapeDtypeStruct((TILE, slots * PAIR), jnp.bfloat16),
        in_specs=[smem_spec()] * 2
        + [
            head_block(lambda i: query_at + i),
            head_block(lambda i: i // 2 * 4 + i % 2),
            head_block(lambda i: i // 2 * 4 + i % 2 + 2),
        ]
        + [pl.BlockSpec((PAIR_MOST, BLOCK, 2 * DH), lambda i: (i // 2, 0, 0))] * (seq_count - 1),
        out_specs=head_block(lambda i: i),
        scratch_shapes=[
            pltpu.VMEM((most_blocks * BLOCK, DH), jnp.bfloat16),
            pltpu.VMEM((most_blocks * BLOCK, DH), jnp.bfloat16),
            pltpu.VMEM((TILE, DH), jnp.float32),
            pltpu.VMEM((TILE, DH), jnp.float32),
            pltpu.VMEM((TILE, DH), jnp.float32),
        ],
        compiler_params=pltpu.CompilerParams(vmem_limit_bytes=VMEM_LIMIT),
        cost_estimate=pl.CostEstimate(
            flops=slots * 2 * TILE * 2 * TILE * DH * 4,
            bytes_accessed=slots * 3 * 1024 * 1024,
            transcendentals=slots * 2 * TILE * 2 * TILE,
        ),
        name="attend",
    )(places, counts, queries, tile, tile, *blocks)


def lay_kernel(groups, table_ref, *refs):
    out_ref = refs[-1]
    rank = pl.program_id(0)
    local_pairs = sum(len(group) for group in groups)
    for group, ref in zip(groups, refs[:-1]):
        for at, pair in enumerate(group):
            column = table_ref[rank * local_pairs + pair] * PAIR
            out_ref[:, pl.ds(pl.multiple_of(column, PAIR), PAIR)] = ref[
                0, :, at * PAIR : (at + 1) * PAIR
            ]


def lay_out(table, stages, groups):
    head_count, rows = stages[0].shape[:2]
    return pl.pallas_call(
        functools.partial(lay_kernel, groups),
        grid=(head_count,),
        out_shape=jax.ShapeDtypeStruct((rows, HEADS * DH), jnp.bfloat16),
        in_specs=[smem_spec()]
        + [pl.BlockSpec((1, rows, len(group) * PAIR), lambda i: (i, 0, 0)) for group in groups],
        out_specs=pl.BlockSpec((rows, HEADS * DH), lambda i: (0, 0)),
        compiler_params=pltpu.CompilerParams(vmem_limit_bytes=VMEM_LIMIT),
        cost_estimate=pl.CostEstimate(
            flops=0, bytes_accessed=rows * HEADS * DH * 4, transcendentals=0
        ),
        name="lay_out",
    )(table, *stages)


def on_device(query_rows, key_rows, value_rows, block_lists, block_counts):
    head_count = lax.axis_size("head")
    seq_count = lax.axis_size("seq")
    seq_rank = lax.axis_index("seq")
    head_rank = lax.axis_index("head")
    rows = query_rows.shape[0]
    local_pairs = HEADS // 2 // head_count
    table = jnp.arange(HEADS // 2, dtype=jnp.int32)
    groups = [[0], list(range(1, local_pairs - 1)), [local_pairs - 1]]
    groups = [group for group in groups if group] if local_pairs > 1 else [[0]]

    lists = block_lists.reshape(-1)
    counts = block_counts.reshape(-1)
    wanted = [shifted(lists, "seq", (seq_count - step) % seq_count) for step in range(1, seq_count)]

    def exchanged(array):
        return lax.all_to_all(array, "head", split_axis=0, concat_axis=0, tiled=True)

    tiles = []
    for group in groups:
        parts = [(array, pair) for pair in group for array in (key_rows, value_rows)]
        query_at = 2 * len(parts)
        if group is groups[-1]:
            parts += [(query_rows, pair) for pair in range(local_pairs)]
        tile = exchanged(gather_columns(table, parts, head_count, local_pairs))
        tile = tile.reshape(TILE, len(parts) * PAIR)
        mine = lax.dynamic_slice_in_dim(table, head_rank * local_pairs + group[0], len(group))
        places = jnp.concatenate([jnp.stack([seq_rank, head_rank]).astype(jnp.int32), mine])
        picked = pick_blocks(places, counts, wanted, tile, len(group))
        blocks = [shifted(picked[step - 1], "seq", step) for step in range(1, seq_count)]
        tiles.append((places, tile, blocks))
    queries = tile

    stages = []
    for group, (places, tile, blocks) in zip(groups, tiles):
        out = attend(
            places, counts, queries, query_at + 2 * group[0], tile, blocks, len(group)
        )
        stages.append(exchanged(out.reshape(head_count, rows, len(group) * PAIR)))
    return lay_out(table, stages, groups)


def solution(mesh):
    in_specs = (
        P(("parts", "seq", "head"), None),
        P(("parts", "seq", "head"), None),
        P(("parts", "seq", "head"), None),
        P("parts", "seq", None, None),
        P("parts", None, None),
    )
    out_specs = P(("parts", "seq", "head"), None)
    return jax.shard_map(
        on_device, mesh=mesh, in_specs=in_specs, out_specs=out_specs, check_vma=False
    )
```

```python
import functools
import math

import jax
import jax.numpy as jnp
from jax import lax
from jax.experimental import pallas as pl
from jax.experimental.pallas import tpu as pltpu
from jax.sharding import PartitionSpec as P

HEADS = 32
DH = 128
BLOCK = 128
MOST = 3
PAIR_MOST = 4
TILE = 768
PAIR = 2 * DH
LIGHT_MOST = 1
VMEM_LIMIT = 60 * 1024 * 1024
SMEM = pltpu.SMEM
BRIEF = pl.CostEstimate(flops=1024, bytes_accessed=1024, transcendentals=0)


def shifted(array, axis, step):
    size = lax.axis_size(axis)
    return lax.ppermute(array, axis, [(i, (i + step) % size) for i in range(size)])


def smem_spec():
    return pl.BlockSpec(memory_space=SMEM)


def one_block(shape):
    return pl.BlockSpec(shape, lambda i, *_: (0,) * len(shape))


def gather_kernel(head_count, place_ref, *refs):
    part_count = len(refs) // head_count - 1
    for step in range(head_count):
        for at in range(part_count):
            refs[head_count * part_count + step][:, at * PAIR : (at + 1) * PAIR] = refs[
                step * part_count + at
            ][...]


def gather_columns(places, parts, head_count, local_pairs):
    rows = parts[0][0].shape[0]

    def column_of(step, pair):
        def index(i, place_ref):
            rank = lax.rem(place_ref[1] + step, head_count)
            return 0, place_ref[2 + rank * local_pairs + pair]

        return index

    return pl.pallas_call(
        functools.partial(gather_kernel, head_count),
        grid_spec=pltpu.PrefetchScalarGridSpec(
            num_scalar_prefetch=1,
            grid=(1,),
            in_specs=[
                pl.BlockSpec((rows, PAIR), column_of(step, pair))
                for step in range(head_count)
                for _, pair in parts
            ],
            out_specs=[one_block((rows, len(parts) * PAIR))] * head_count,
        ),
        out_shape=[jax.ShapeDtypeStruct((rows, len(parts) * PAIR), jnp.bfloat16)] * head_count,
        compiler_params=pltpu.CompilerParams(vmem_limit_bytes=VMEM_LIMIT),
        cost_estimate=BRIEF,
        name="gather_columns",
    )(places, *[array for array, _ in parts] * head_count)


def pick_kernel(head_count, seq_count, first_pair, caps, place_ref, counts_ref, *refs):
    want_refs = refs[: seq_count - 1]
    rows_refs = refs[seq_count - 1 : seq_count - 1 + head_count]
    tile_ref = refs[seq_count - 1 + head_count]
    send_refs = refs[seq_count + head_count :]
    my_seq, my_head = place_ref[0], place_ref[1]
    rows = TILE // head_count
    pair_at = 2 + my_head * (HEADS // 2 // head_count) + first_pair
    for step in range(head_count):
        rank = lax.rem(my_head - step + head_count, head_count)
        place = pl.ds(pl.multiple_of(rank * rows, 16), rows)
        for pair in range(len(caps)):
            for half in range(2):
                base = pair * 2 * PAIR + half * DH
                tile_ref[2 * pair + half, place, :DH] = rows_refs[step][:, base : base + DH]
                tile_ref[2 * pair + half, place, DH:] = rows_refs[step][
                    :, base + PAIR : base + PAIR + DH
                ]
    for step in range(1, seq_count):
        asker = lax.rem(my_seq + step, seq_count)
        for pair, cap in enumerate(caps):
            first = 2 * place_ref[pair_at + pair]
            first_count = counts_ref[(first * seq_count + asker) * seq_count + my_seq]
            both = first_count + counts_ref[((first + 1) * seq_count + asker) * seq_count + my_seq]
            for slot in range(cap):

                @pl.when(slot < both)
                def _():
                    half = jnp.where(slot < first_count, 0, 1)
                    entry = jnp.where(slot < first_count, slot, slot - first_count)
                    entry = jnp.clip(entry, 0, MOST - 1)
                    block = want_refs[step - 1][
                        ((first + half) * seq_count + my_seq) * MOST + entry
                    ]
                    send_refs[step - 1][pair * PAIR_MOST + slot] = tile_ref[
                        2 * pair + half, pl.ds(pl.multiple_of(block * BLOCK, BLOCK), BLOCK), :
                    ]


def pick_blocks(places, counts, wanted, pieces, first_pair, caps):
    slots = len(caps)
    head_count, seq_count = len(pieces), len(wanted) + 1
    out_shape = [jax.ShapeDtypeStruct((2 * slots, TILE, 2 * DH), jnp.bfloat16)]
    out_shape += [
        jax.ShapeDtypeStruct((sum(caps), BLOCK, 2 * DH), jnp.bfloat16)
    ] * (seq_count - 1)
    outs = pl.pallas_call(
        functools.partial(pick_kernel, head_count, seq_count, first_pair, caps),
        out_shape=out_shape,
        grid=(1,),
        in_specs=[smem_spec()] * (seq_count + 1) + [one_block((pieces[0].shape[0], slots * 2 * PAIR))]
        * head_count,
        out_specs=[one_block(shape.shape) for shape in out_shape],
        compiler_params=pltpu.CompilerParams(vmem_limit_bytes=VMEM_LIMIT),
        cost_estimate=BRIEF,
        name="pick_blocks",
    )(places, counts, *wanted, *pieces)
    return outs[0], outs[1:]


GROUP = 3 * BLOCK


def fold(values, combine):
    total = values[:, :DH]
    for start in range(DH, values.shape[1], DH):
        total = combine(total, values[:, start : start + DH])
    return total


def row_top(scores):
    top = jnp.max(fold(scores, jnp.maximum), axis=1, keepdims=True)
    return jnp.broadcast_to(top, (scores.shape[0], DH))


def weigh(scores, top):
    return jnp.concatenate(
        [jnp.exp2(scores[:, at : at + DH] - top) for at in range(0, scores.shape[1], DH)], axis=1
    )


def start_state(queries, keys, values, scale):
    scores = score(queries, keys, scale)
    top = row_top(scores)
    weights = weigh(scores, top)
    mixture = jnp.dot(weights.astype(jnp.bfloat16), values, preferred_element_type=jnp.float32)
    return top, fold(weights, jnp.add), mixture


def score(queries, keys, scale):
    products = lax.dot_general(
        queries, keys, (((1,), (1,)), ((), ())), preferred_element_type=jnp.float32
    )
    return products * scale


SCALE = math.log2(math.e) / math.sqrt(DH)


def fetch_blocks(place_ref, counts_ref, block_refs, k_ref, v_ref, head_count, first_pair):
    seq_count = len(block_refs) + 1
    my_seq = place_ref[0]
    turn = pl.program_id(0)
    half = lax.rem(turn, 2)
    pair_at = 2 + place_ref[1] * (HEADS // 2 // head_count) + first_pair
    first = 2 * place_ref[pair_at + turn // 2]
    slot_most = block_refs[0].shape[0] - 1
    used = jnp.int32(0)
    for step in range(1, seq_count):
        holder = lax.rem(my_seq - step + seq_count, seq_count)
        first_count = counts_ref[(first * seq_count + my_seq) * seq_count + holder]
        second_count = counts_ref[((first + 1) * seq_count + my_seq) * seq_count + holder]
        count = jnp.where(half == 0, first_count, second_count)
        start = jnp.where(half == 0, 0, first_count) + turn // 2 * PAIR_MOST
        for entry in range(MOST):

            @pl.when(entry < count)
            def _():
                place = pl.ds(pl.multiple_of((used + entry) * BLOCK, BLOCK), BLOCK)
                slot = jnp.minimum(start + entry, slot_most)
                k_ref[place, :] = block_refs[step - 1][slot, :, :DH]
                v_ref[place, :] = block_refs[step - 1][slot, :, DH:]

        used = used + count
    return used


def visit_blocks(used, q_ref, k_ref, v_ref, top_ref, sum_ref, mix_ref):
    def visit(group, carry):
        place = pl.ds(pl.multiple_of(group * GROUP, GROUP), GROUP)
        column = lax.broadcasted_iota(jnp.int32, (1, GROUP), 1) + group * GROUP
        bias = jnp.where(column < used * BLOCK, 0.0, -jnp.inf)
        scores = score(q_ref[...], k_ref[place, :], SCALE) + bias
        old_top = top_ref[...]
        top = jnp.maximum(old_top, row_top(scores))
        weights = weigh(scores, top)
        rescale = jnp.exp2(old_top - top)
        top_ref[...] = top
        sum_ref[...] = sum_ref[...] * rescale + fold(weights, jnp.add)
        mix_ref[...] = mix_ref[...] * rescale + jnp.dot(
            weights.astype(jnp.bfloat16), v_ref[place, :], preferred_element_type=jnp.float32
        )
        return carry

    lax.fori_loop(0, (used + 2) // 3, visit, 0)


def clear_blocks(k_ref, v_ref):
    @pl.when(pl.program_id(0) == 0)
    def _():
        k_ref[...] = jnp.zeros_like(k_ref)
        v_ref[...] = jnp.zeros_like(v_ref)


def join_pieces(query_refs, q_ref):
    rows = TILE // len(query_refs)
    for step, ref in enumerate(query_refs):
        q_ref[step * rows : (step + 1) * rows, :] = ref[...]


def split_result(out_refs, sum_ref, mix_ref):
    rows = TILE // len(out_refs)
    for step, ref in enumerate(out_refs):
        span = slice(step * rows, (step + 1) * rows)
        total = jnp.sum(sum_ref[span, :], axis=1, keepdims=True)
        ref[...] = (mix_ref[span, :] / total).astype(jnp.bfloat16)


def attend_kernel(head_count, seq_count, first_pair, place_ref, counts_ref, tile_ref, *refs):
    query_refs, refs = refs[:head_count], refs[head_count:]
    block_refs, refs = refs[: seq_count - 1], refs[seq_count - 1 :]
    out_refs, refs = refs[:head_count], refs[head_count:]
    q_ref, k_ref, v_ref, top_ref, sum_ref, mix_ref = refs
    clear_blocks(k_ref, v_ref)
    join_pieces(query_refs, q_ref)
    used = fetch_blocks(place_ref, counts_ref, block_refs, k_ref, v_ref, head_count, first_pair)
    top_ref[...], sum_ref[...], mix_ref[...] = start_state(
        q_ref[...], tile_ref[0, :, :DH], tile_ref[0, :, DH:], SCALE
    )
    visit_blocks(used, q_ref, k_ref, v_ref, top_ref, sum_ref, mix_ref)
    split_result(out_refs, sum_ref, mix_ref)


def own_kernel(head_count, tile_ref, *refs):
    query_refs, (top_ref, sum_ref, mix_ref, q_ref) = refs[:head_count], refs[head_count:]
    join_pieces(query_refs, q_ref)
    top_ref[0], sum_ref[0], mix_ref[0] = start_state(
        q_ref[...], tile_ref[0, :, :DH], tile_ref[0, :, DH:], SCALE
    )


def far_kernel(head_count, seq_count, first_pair, place_ref, counts_ref, *refs):
    old_top_ref, old_sum_ref, old_mix_ref = refs[:3]
    query_refs, refs = refs[3 : 3 + head_count], refs[3 + head_count :]
    block_refs, refs = refs[: seq_count - 1], refs[seq_count - 1 :]
    out_refs, refs = refs[:head_count], refs[head_count:]
    q_ref, k_ref, v_ref, top_ref, sum_ref, mix_ref = refs
    clear_blocks(k_ref, v_ref)
    join_pieces(query_refs, q_ref)
    used = fetch_blocks(place_ref, counts_ref, block_refs, k_ref, v_ref, head_count, first_pair)
    top_ref[...], sum_ref[...], mix_ref[...] = old_top_ref[0], old_sum_ref[0], old_mix_ref[0]
    visit_blocks(used, q_ref, k_ref, v_ref, top_ref, sum_ref, mix_ref)
    split_result(out_refs, sum_ref, mix_ref)


def state_spec():
    return pl.BlockSpec((1, TILE, DH), lambda i: (i, 0, 0))


def tile_spec():
    return pl.BlockSpec((1, TILE, 2 * DH), lambda i: (i, 0, 0))


def query_specs(queries, query_at):
    return [pl.BlockSpec((piece.shape[0], DH), lambda i: (0, query_at + i)) for piece in queries]


def attention_call(kernel, name, slots, seq_count, operands, in_specs, head_count):
    most_blocks = -(-(seq_count - 1) * MOST // 3) * 3
    rows = TILE // head_count
    return pl.pallas_call(
        kernel,
        grid=(2 * slots,),
        out_shape=[jax.ShapeDtypeStruct((rows, slots * PAIR), jnp.bfloat16)] * head_count,
        in_specs=in_specs,
        out_specs=[pl.BlockSpec((rows, DH), lambda i: (0, i))] * head_count,
        scratch_shapes=[
            pltpu.VMEM((TILE, DH), jnp.bfloat16),
            pltpu.VMEM((most_blocks * BLOCK, DH), jnp.bfloat16),
            pltpu.VMEM((most_blocks * BLOCK, DH), jnp.bfloat16),
            pltpu.VMEM((TILE, DH), jnp.float32),
            pltpu.VMEM((TILE, DH), jnp.float32),
            pltpu.VMEM((TILE, DH), jnp.float32),
        ],
        compiler_params=pltpu.CompilerParams(vmem_limit_bytes=VMEM_LIMIT),
        cost_estimate=BRIEF,
        name=name,
    )(*operands)


def attend(places, counts, tile_pairs, queries, query_at, blocks, first_pair, slots):
    head_count, seq_count = len(queries), len(blocks) + 1
    return attention_call(
        functools.partial(attend_kernel, head_count, seq_count, first_pair),
        "attend",
        slots,
        seq_count,
        (places, counts, tile_pairs, *queries, *blocks),
        [smem_spec()] * 2
        + [tile_spec()]
        + query_specs(queries, query_at)
        + [one_block(block.shape) for block in blocks],
        head_count,
    )


def attend_own(tile_pairs, queries, query_at, slots):
    head_count = len(queries)
    return pl.pallas_call(
        functools.partial(own_kernel, head_count),
        grid=(2 * slots,),
        out_shape=[jax.ShapeDtypeStruct((2 * slots, TILE, DH), jnp.float32)] * 3,
        in_specs=[tile_spec()] + query_specs(queries, query_at),
        out_specs=[state_spec()] * 3,
        scratch_shapes=[pltpu.VMEM((TILE, DH), jnp.bfloat16)],
        compiler_params=pltpu.CompilerParams(vmem_limit_bytes=VMEM_LIMIT),
        cost_estimate=BRIEF,
        name="attend_own",
    )(tile_pairs, *queries)


def attend_far(places, counts, state, queries, query_at, blocks, first_pair, slots):
    head_count, seq_count = len(queries), len(blocks) + 1
    return attention_call(
        functools.partial(far_kernel, head_count, seq_count, first_pair),
        "attend_far",
        slots,
        seq_count,
        (places, counts, *state, *queries, *blocks),
        [smem_spec()] * 2
        + [state_spec()] * 3
        + query_specs(queries, query_at)
        + [one_block(block.shape) for block in blocks],
        head_count,
    )


def lay_kernel(groups, head_count, place_ref, *refs):
    out_ref = refs[-1]
    local_pairs = HEADS // 2 // head_count
    for number, group in enumerate(groups):
        for step in range(head_count):
            rank = lax.rem(place_ref[1] - step + head_count, head_count)
            for at, pair in enumerate(group):
                column = place_ref[2 + rank * local_pairs + pair] * PAIR
                out_ref[:, pl.ds(pl.multiple_of(column, PAIR), PAIR)] = refs[
                    number * head_count + step
                ][:, at * PAIR : (at + 1) * PAIR]


def lay_out(places, stages, groups):
    head_count = len(stages[0])
    rows = stages[0][0].shape[0]
    flat = [piece for stage in stages for piece in stage]
    return pl.pallas_call(
        functools.partial(lay_kernel, groups, head_count),
        grid=(1,),
        out_shape=jax.ShapeDtypeStruct((rows, HEADS * DH), jnp.bfloat16),
        in_specs=[smem_spec()] + [one_block(piece.shape) for piece in flat],
        out_specs=one_block((rows, HEADS * DH)),
        compiler_params=pltpu.CompilerParams(vmem_limit_bytes=VMEM_LIMIT),
        cost_estimate=BRIEF,
        name="lay_out",
    )(places, *flat)


def after(value, *others):
    return lax.optimization_barrier((value, others))[0]


def place_pairs(block_counts, head_count, local_pairs):
    pair_count = HEADS // 2
    listed = jnp.sum(block_counts.reshape(pair_count, 2, *block_counts.shape[1:]), axis=1)
    total = jnp.sum(listed, axis=(1, 2))
    most = jnp.max(listed, axis=(1, 2))
    pairs = jnp.arange(pair_count, dtype=jnp.int32)
    ahead = (total[None, :] > total[:, None]) | (
        (total[None, :] == total[:, None]) & (pairs[None, :] < pairs[:, None])
    )
    order = jnp.sum(ahead.astype(jnp.int32), axis=1)
    place = order % head_count * local_pairs + order // head_count
    hit = place[None, :] == pairs[:, None]
    table = jnp.sum(jnp.where(hit, pairs[None, :], 0), axis=1)
    return table, jnp.where(order >= 3 * head_count, most, 0)


def on_device(query_rows, key_rows, value_rows, block_lists, block_counts):
    head_count = lax.axis_size("head")
    seq_count = lax.axis_size("seq")
    part_count = lax.axis_size("parts")
    local_pairs = HEADS // 2 // head_count
    ranks = jnp.stack([lax.axis_index("seq"), lax.axis_index("head")]).astype(jnp.int32)
    table, light_most = place_pairs(block_counts, head_count, local_pairs)
    places = jnp.concatenate([ranks, table])
    groups = [[0], list(range(2, local_pairs)), [1]]
    groups = [group for group in groups if group and group[-1] < local_pairs]

    sources, query_from = [], {}
    for number, group in enumerate(groups):
        parts = [(array, pair) for pair in group for array in (key_rows, value_rows)]
        if len(groups) == 1 or number == 1:
            asked = [0]
        elif number == 0:
            asked = []
        else:
            asked = [1, 2]
        for other in asked:
            query_from[other] = (number, len(parts) * 2)
            parts += [(query_rows, pair) for pair in groups[other]]
        sources.append(gather_columns(places, parts, head_count, local_pairs))

    def spread(source):
        return [source[0]] + [shifted(source[step], "head", step) for step in range(1, head_count)]

    def returned(outs):
        return [outs[0]] + [
            shifted(outs[head_count - step], "head", step) for step in range(1, head_count)
        ]

    def passed_on(picked):
        return [shifted(picked[step - 1], "seq", step) for step in range(1, seq_count)]

    pieces = [spread(sources[0])]
    lists, counts = after((block_lists, block_counts), sources[0])
    lists, counts = lists.reshape(-1), counts.reshape(-1)
    wanted = [shifted(lists, "seq", (seq_count - step) % seq_count) for step in range(1, seq_count)]

    def pick(number, arrived, light):
        caps = [light if pair >= 3 else PAIR_MOST for pair in groups[number]]
        return pick_blocks(places, counts, wanted, arrived, groups[number][0], caps)

    def whole(number, tile_pairs, blocks):
        source, at = query_from[number]
        group = groups[number]
        return attend(
            places, counts, tile_pairs, pieces[source], at, blocks, group[0], len(group)
        )

    if len(groups) == 1:
        tile_pairs, picked = pick(0, pieces[0], PAIR_MOST)
        return lay_out(places, [returned(whole(0, tile_pairs, passed_on(picked)))], groups)

    pieces.append(spread(after(sources[1], pieces[0], wanted, counts)))
    tile_pairs, picked = pick(0, pieces[0], PAIR_MOST)
    blocks = passed_on(picked)
    light_most = after(jnp.max(after(light_most, sources[0])), pieces[1][1])
    for step in range(1, part_count):
        light_most = jnp.maximum(light_most, shifted(light_most[None], "parts", step)[0])
    first = (tile_pairs, blocks)
    light_most, first, arrived, third = lax.optimization_barrier(
        (light_most, first, pieces[1], sources[2])
    )

    def finish(light, first, arrived, third):
        pieces[1] = arrived
        tile_pairs, picked = pick(1, arrived, light)
        pieces[2:] = [spread(after(third, picked))]
        second = (tile_pairs, passed_on(picked))
        outs = whole(0, *after(first, picked))
        arrived = after(pieces[2], outs, second[1])
        tile_pairs, picked = pick(2, arrived, light)
        results = [returned(outs)]
        blocks = passed_on(picked)
        results.append(returned(whole(1, *after(second, picked))))
        source, at = query_from[2]
        state = attend_own(tile_pairs, pieces[source], at, 1)
        state = after(state, results[0], results[1][0])
        outs = attend_far(places, counts, state, pieces[source], at, blocks, groups[2][0], 1)
        results.append(returned(outs))
        return lay_out(places, results, groups)

    if max(max(group) for group in groups) < 3:
        return finish(PAIR_MOST, first, arrived, third)
    return lax.cond(
        light_most > LIGHT_MOST,
        functools.partial(finish, PAIR_MOST),
        functools.partial(finish, LIGHT_MOST),
        first,
        arrived,
        third,
    )


def solution(mesh):
    in_specs = (
        P(("parts", "seq", "head"), None),
        P(("parts", "seq", "head"), None),
        P(("parts", "seq", "head"), None),
        P("parts", "seq", None, None),
        P("parts", None, None),
    )
    out_specs = P(("parts", "seq", "head"), None)
    return jax.shard_map(
        on_device, mesh=mesh, in_specs=in_specs, out_specs=out_specs, check_vma=False
    )
```

```python
import functools
import math

import jax
import jax.numpy as jnp
from jax import lax
from jax.experimental import pallas as pl
from jax.experimental.pallas import tpu as pltpu
from jax.sharding import PartitionSpec as P

HEADS = 32
DH = 128
BLOCK = 128
MOST = 3
PAIR_MOST = 4
TILE = 768
PAIR = 2 * DH
LIGHT_MOST = 1
VMEM_LIMIT = 60 * 1024 * 1024 + 448 * 1024
SMEM = pltpu.SMEM
LONG = pl.CostEstimate(flops=2 * 10**11, bytes_accessed=2 * 10**9, transcendentals=0)
BRIEF = pl.CostEstimate(flops=1024, bytes_accessed=1024, transcendentals=0)


def paired(size):
    return size & (size - 1) == 0


def ahead(rank, step, size):
    return rank ^ step if paired(size) else (rank + step) % size


def behind(rank, step, size):
    return rank ^ step if paired(size) else (rank + size - step) % size


def backward(step, size):
    return step if paired(size) else size - step


def shifted(array, axis, step):
    size = lax.axis_size(axis)
    return lax.ppermute(array, axis, [(i, ahead(i, step, size)) for i in range(size)])


def turned(array, axis, step):
    size = lax.axis_size(axis)
    return lax.ppermute(array, axis, [(i, (i + step) % size) for i in range(size)])


def smem_spec():
    return pl.BlockSpec(memory_space=SMEM)


def one_block(shape):
    return pl.BlockSpec(shape, lambda i, *_: (0,) * len(shape))


def gather_kernel(head_count, place_ref, *refs):
    part_count = len(refs) // head_count - 1
    for step in range(head_count):
        for at in range(part_count):
            refs[head_count * part_count + step][:, at * PAIR : (at + 1) * PAIR] = refs[
                step * part_count + at
            ][...]


def gather_columns(places, parts, head_count, local_pairs):
    rows = parts[0][0].shape[0]

    def column_of(step, pair):
        def index(i, place_ref):
            rank = ahead(place_ref[1], step, head_count)
            return 0, place_ref[2 + rank * local_pairs + pair]

        return index

    return pl.pallas_call(
        functools.partial(gather_kernel, head_count),
        grid_spec=pltpu.PrefetchScalarGridSpec(
            num_scalar_prefetch=1,
            grid=(1,),
            in_specs=[
                pl.BlockSpec((rows, PAIR), column_of(step, pair))
                for step in range(head_count)
                for _, pair in parts
            ],
            out_specs=[one_block((rows, len(parts) * PAIR))] * head_count,
        ),
        out_shape=[jax.ShapeDtypeStruct((rows, len(parts) * PAIR), jnp.bfloat16)] * head_count,
        compiler_params=pltpu.CompilerParams(vmem_limit_bytes=VMEM_LIMIT),
        cost_estimate=BRIEF,
        name="gather_columns",
    )(places, *[array for array, _ in parts] * head_count)


def pick_kernel(head_count, seq_count, first_pair, caps, place_ref, counts_ref, *refs):
    want_refs = refs[: seq_count - 1]
    rows_refs = refs[seq_count - 1 : seq_count - 1 + head_count]
    tile_ref = refs[seq_count - 1 + head_count]
    send_refs = refs[seq_count + head_count :]
    my_seq, my_head = place_ref[0], place_ref[1]
    rows = TILE // head_count
    pair_at = 2 + my_head * (HEADS // 2 // head_count) + first_pair
    for step in range(head_count):
        rank = behind(my_head, step, head_count)
        place = pl.ds(pl.multiple_of(rank * rows, 16), rows)
        for pair in range(len(caps)):
            for half in range(2):
                base = pair * 2 * PAIR + half * DH
                tile_ref[2 * pair + half, place, :DH] = rows_refs[step][:, base : base + DH]
                tile_ref[2 * pair + half, place, DH:] = rows_refs[step][
                    :, base + PAIR : base + PAIR + DH
                ]
    for step in range(1, seq_count):
        asker = lax.rem(my_seq + step, seq_count)
        for pair, cap in enumerate(caps):
            first = 2 * place_ref[pair_at + pair]
            first_count = counts_ref[(first * seq_count + asker) * seq_count + my_seq]
            both = first_count + counts_ref[((first + 1) * seq_count + asker) * seq_count + my_seq]
            for slot in range(cap):

                @pl.when(slot < both)
                def _():
                    half = jnp.where(slot < first_count, 0, 1)
                    entry = jnp.where(slot < first_count, slot, slot - first_count)
                    entry = jnp.clip(entry, 0, MOST - 1)
                    block = want_refs[step - 1][
                        ((first + half) * seq_count + my_seq) * MOST + entry
                    ]
                    send_refs[step - 1][pair * PAIR_MOST + slot] = tile_ref[
                        2 * pair + half, pl.ds(pl.multiple_of(block * BLOCK, BLOCK), BLOCK), :
                    ]


def pick_blocks(places, counts, wanted, pieces, first_pair, caps):
    slots = len(caps)
    head_count, seq_count = len(pieces), len(wanted) + 1
    out_shape = [jax.ShapeDtypeStruct((2 * slots, TILE, 2 * DH), jnp.bfloat16)]
    out_shape += [
        jax.ShapeDtypeStruct((sum(caps), BLOCK, 2 * DH), jnp.bfloat16)
    ] * (seq_count - 1)
    outs = pl.pallas_call(
        functools.partial(pick_kernel, head_count, seq_count, first_pair, caps),
        out_shape=out_shape,
        grid=(1,),
        in_specs=[smem_spec()] * (seq_count + 1) + [one_block((pieces[0].shape[0], slots * 2 * PAIR))]
        * head_count,
        out_specs=[one_block(shape.shape) for shape in out_shape],
        compiler_params=pltpu.CompilerParams(vmem_limit_bytes=VMEM_LIMIT),
        cost_estimate=BRIEF,
        name="pick_blocks",
    )(places, counts, *wanted, *pieces)
    return outs[0], outs[1:]


GROUP = 3 * BLOCK


def fold(values, combine):
    total = values[:, :DH]
    for start in range(DH, values.shape[1], DH):
        total = combine(total, values[:, start : start + DH])
    return total


def row_top(scores):
    top = jnp.max(fold(scores, jnp.maximum), axis=1, keepdims=True)
    return jnp.broadcast_to(top, (scores.shape[0], DH))


def weigh(scores, top):
    return jnp.concatenate(
        [jnp.exp2(scores[:, at : at + DH] - top) for at in range(0, scores.shape[1], DH)], axis=1
    )


def start_state(queries, tile_ref, top_ref, sum_ref, mix_ref):
    for start in range(0, TILE, GROUP):
        scores = score(queries, tile_ref[0, start : start + GROUP, :DH], SCALE)
        values = tile_ref[0, start : start + GROUP, DH:]
        add_group(scores, values, top_ref, sum_ref, mix_ref, start == 0)


def add_group(scores, values, top_ref, sum_ref, mix_ref, first):
    top = row_top(scores)
    if not first:
        old_top = top_ref[...]
        top = jnp.maximum(old_top, top)
    weights = weigh(scores, top)
    sums = fold(weights, jnp.add)
    mixture = jnp.dot(weights.astype(jnp.bfloat16), values, preferred_element_type=jnp.float32)
    if not first:
        rescale = jnp.exp2(old_top - top)
        sums = sum_ref[...] * rescale + sums
        mixture = mix_ref[...] * rescale + mixture
    top_ref[...] = top
    sum_ref[...] = sums
    mix_ref[...] = mixture


def score(queries, keys, scale):
    products = lax.dot_general(
        queries, keys, (((1,), (1,)), ((), ())), preferred_element_type=jnp.float32
    )
    return products * scale


SCALE = math.log2(math.e) / math.sqrt(DH)


def block_copies(place_ref, counts_ref, block_refs, kv_ref, sems, head_count, first_pair, turn):
    seq_count = len(block_refs) + 1
    my_seq = place_ref[0]
    half = lax.rem(turn, 2)
    pair_at = 2 + place_ref[1] * (HEADS // 2 // head_count) + first_pair
    first = 2 * place_ref[pair_at + turn // 2]
    slot_most = block_refs[0].shape[0] - 1
    used = jnp.int32(0)
    copies = []
    for step in range(1, seq_count):
        holder = lax.rem(my_seq - step + seq_count, seq_count)
        first_count = counts_ref[(first * seq_count + my_seq) * seq_count + holder]
        second_count = counts_ref[((first + 1) * seq_count + my_seq) * seq_count + holder]
        count = jnp.where(half == 0, first_count, second_count)
        start = jnp.where(half == 0, 0, first_count) + turn // 2 * PAIR_MOST
        for entry in range(MOST):
            place = pl.ds(pl.multiple_of((used + entry) * BLOCK, BLOCK), BLOCK)
            copy = pltpu.make_async_copy(
                block_refs[step - 1].at[jnp.minimum(start + entry, slot_most)],
                kv_ref.at[half, place],
                sems.at[half, len(copies)],
            )
            copies.append((entry < count, copy))
        used = used + count
    return copies, used


def start_copies(copies, also=True):
    for needed, copy in copies:
        pl.when(needed & also)(copy.start)


def wait_copies(copies):
    for needed, copy in copies:
        pl.when(needed)(copy.wait)


def fetch_blocks(place_ref, counts_ref, block_refs, kv_ref, sems, head_count, first_pair):
    turn, turns = pl.program_id(0), pl.num_programs(0)
    shared = (place_ref, counts_ref, block_refs, kv_ref, sems, head_count, first_pair)
    copies, used = block_copies(*shared, turn)

    @pl.when(turn == 0)
    def _():
        kv_ref[...] = jnp.zeros_like(kv_ref)
        start_copies(copies)

    later, _ = block_copies(*shared, jnp.minimum(turn + 1, turns - 1))
    start_copies(later, turn + 1 < turns)
    return copies, used


def visit_blocks(used, q_ref, kv_ref, top_ref, sum_ref, mix_ref):
    half = lax.rem(pl.program_id(0), 2)

    def visit(group, carry):
        place = pl.ds(pl.multiple_of(group * GROUP, GROUP), GROUP)
        column = lax.broadcasted_iota(jnp.int32, (1, GROUP), 1) + group * GROUP
        bias = jnp.where(column < used * BLOCK, 0.0, -jnp.inf)
        scores = score(q_ref[...], kv_ref[half, place, :DH], SCALE) + bias
        add_group(scores, kv_ref[half, place, DH:], top_ref, sum_ref, mix_ref, False)
        return carry

    lax.fori_loop(0, (used + 2) // 3, visit, 0)


def join_pieces(query_refs, q_ref):
    rows = TILE // len(query_refs)
    for step, ref in enumerate(query_refs):
        q_ref[step * rows : (step + 1) * rows, :] = ref[...]


def split_result(out_refs, sum_ref, mix_ref):
    rows = TILE // len(out_refs)
    for step, ref in enumerate(out_refs):
        span = slice(step * rows, (step + 1) * rows)
        total = jnp.sum(sum_ref[span, :], axis=1, keepdims=True)
        ref[...] = (mix_ref[span, :] / total).astype(jnp.bfloat16)


def attend_kernel(head_count, seq_count, first_pair, joined, place_ref, counts_ref, tile_ref, *refs):
    query_refs, refs = refs[:head_count], refs[head_count:]
    block_refs, refs = refs[: seq_count - 1], refs[seq_count - 1 :]
    refs = refs[head_count:] if joined else refs
    out_refs, refs = refs[:head_count], refs[head_count:]
    q_ref, kv_ref, top_ref, sum_ref, mix_ref, sems = refs
    join_pieces(query_refs, q_ref)
    copies, used = fetch_blocks(
        place_ref, counts_ref, block_refs, kv_ref, sems, head_count, first_pair
    )
    start_state(q_ref[...], tile_ref, top_ref, sum_ref, mix_ref)
    wait_copies(copies)
    visit_blocks(used, q_ref, kv_ref, top_ref, sum_ref, mix_ref)
    split_result(out_refs, sum_ref, mix_ref)


def own_kernel(head_count, tile_ref, *refs):
    query_refs, (top_ref, sum_ref, mix_ref, q_ref) = refs[:head_count], refs[head_count:]
    join_pieces(query_refs, q_ref)
    start_state(q_ref[...], tile_ref, top_ref.at[0], sum_ref.at[0], mix_ref.at[0])


def far_kernel(head_count, seq_count, first_pair, place_ref, counts_ref, *refs):
    old_top_ref, old_sum_ref, old_mix_ref = refs[:3]
    query_refs, refs = refs[3 : 3 + head_count], refs[3 + head_count :]
    block_refs, refs = refs[: seq_count - 1], refs[seq_count - 1 :]
    out_refs, refs = refs[:head_count], refs[head_count:]
    q_ref, kv_ref, top_ref, sum_ref, mix_ref, sems = refs
    join_pieces(query_refs, q_ref)
    copies, used = fetch_blocks(
        place_ref, counts_ref, block_refs, kv_ref, sems, head_count, first_pair
    )
    top_ref[...], sum_ref[...], mix_ref[...] = old_top_ref[0], old_sum_ref[0], old_mix_ref[0]
    wait_copies(copies)
    visit_blocks(used, q_ref, kv_ref, top_ref, sum_ref, mix_ref)
    split_result(out_refs, sum_ref, mix_ref)


def state_spec():
    return pl.BlockSpec((1, TILE, DH), lambda i: (i, 0, 0))


def tile_spec():
    return pl.BlockSpec((1, TILE, 2 * DH), lambda i: (i, 0, 0))


def query_specs(queries, query_at):
    return [pl.BlockSpec((piece.shape[0], DH), lambda i: (0, query_at + i)) for piece in queries]


def attention_call(kernel, name, slots, seq_count, operands, in_specs, head_count, width, into):
    written = into[1] if into else 0
    operands = list(operands) + list(into[0] if into else [])
    aliases = {len(operands) - head_count + i: i for i in range(head_count)} if into else {}
    in_specs = in_specs + ([pl.BlockSpec(memory_space=pltpu.HBM)] * head_count if into else [])
    most_blocks = -(-(seq_count - 1) * MOST // 3) * 3
    rows = TILE // head_count
    return pl.pallas_call(
        kernel,
        grid=(2 * slots,),
        out_shape=[jax.ShapeDtypeStruct((rows, width * PAIR), jnp.bfloat16)] * head_count,
        in_specs=in_specs,
        out_specs=[pl.BlockSpec((rows, DH), lambda i: (0, 2 * written + i))] * head_count,
        scratch_shapes=[
            pltpu.VMEM((TILE, DH), jnp.bfloat16),
            pltpu.VMEM((2, most_blocks * BLOCK, 2 * DH), jnp.bfloat16),
            pltpu.VMEM((TILE, DH), jnp.float32),
            pltpu.VMEM((TILE, DH), jnp.float32),
            pltpu.VMEM((TILE, DH), jnp.float32),
            pltpu.SemaphoreType.DMA((2, MOST * (seq_count - 1))),
        ],
        input_output_aliases=aliases,
        compiler_params=pltpu.CompilerParams(vmem_limit_bytes=VMEM_LIMIT),
        cost_estimate=LONG if name == "attend_far" else BRIEF,
        name=name,
    )(*operands)


def attend(
    places, counts, tile_pairs, queries, query_at, blocks, first_pair, slots, width, into=None
):
    head_count, seq_count = len(queries), len(blocks) + 1
    return attention_call(
        functools.partial(attend_kernel, head_count, seq_count, first_pair, bool(into)),
        "attend",
        slots,
        seq_count,
        (places, counts, tile_pairs, *queries, *blocks),
        [smem_spec()] * 2
        + [tile_spec()]
        + query_specs(queries, query_at)
        + [pl.BlockSpec(memory_space=pltpu.HBM)] * len(blocks),
        head_count,
        width,
        into,
    )


def attend_own(tile_pairs, queries, query_at, slots):
    head_count = len(queries)
    return pl.pallas_call(
        functools.partial(own_kernel, head_count),
        grid=(2 * slots,),
        out_shape=[jax.ShapeDtypeStruct((2 * slots, TILE, DH), jnp.float32)] * 3,
        in_specs=[tile_spec()] + query_specs(queries, query_at),
        out_specs=[state_spec()] * 3,
        scratch_shapes=[pltpu.VMEM((TILE, DH), jnp.bfloat16)],
        compiler_params=pltpu.CompilerParams(vmem_limit_bytes=VMEM_LIMIT),
        cost_estimate=BRIEF,
        name="attend_own",
    )(tile_pairs, *queries)


def attend_far(places, counts, state, queries, query_at, blocks, first_pair, slots):
    head_count, seq_count = len(queries), len(blocks) + 1
    return attention_call(
        functools.partial(far_kernel, head_count, seq_count, first_pair),
        "attend_far",
        slots,
        seq_count,
        (places, counts, *state, *queries, *blocks),
        [smem_spec()] * 2
        + [state_spec()] * 3
        + query_specs(queries, query_at)
        + [pl.BlockSpec(memory_space=pltpu.HBM)] * len(blocks),
        head_count,
        slots,
        None,
    )


def lay_kernel(groups, head_count, place_ref, *refs):
    out_ref = refs[-1]
    local_pairs = HEADS // 2 // head_count
    for number, group in enumerate(groups):
        for step in range(head_count):
            rank = behind(place_ref[1], step, head_count)
            for at, pair in enumerate(group):
                column = place_ref[2 + rank * local_pairs + pair] * PAIR
                out_ref[:, pl.ds(pl.multiple_of(column, PAIR), PAIR)] = refs[
                    number * head_count + step
                ][:, at * PAIR : (at + 1) * PAIR]


def lay_out(places, stages, groups):
    head_count = len(stages[0])
    rows = stages[0][0].shape[0]
    flat = [piece for stage in stages for piece in stage]
    return pl.pallas_call(
        functools.partial(lay_kernel, groups, head_count),
        grid=(1,),
        out_shape=jax.ShapeDtypeStruct((rows, HEADS * DH), jnp.bfloat16),
        in_specs=[smem_spec()] + [one_block(piece.shape) for piece in flat],
        out_specs=one_block((rows, HEADS * DH)),
        compiler_params=pltpu.CompilerParams(vmem_limit_bytes=VMEM_LIMIT),
        cost_estimate=BRIEF,
        name="lay_out",
    )(places, *flat)


def after(value, *others):
    return lax.optimization_barrier((value, others))[0]


def place_pairs(block_counts, head_count, local_pairs):
    pair_count = HEADS // 2
    listed = jnp.sum(block_counts.reshape(pair_count, 2, *block_counts.shape[1:]), axis=1)
    total = jnp.sum(listed, axis=(1, 2))
    most = jnp.max(listed, axis=(1, 2))
    pairs = jnp.arange(pair_count, dtype=jnp.int32)
    ahead = (total[None, :] > total[:, None]) | (
        (total[None, :] == total[:, None]) & (pairs[None, :] < pairs[:, None])
    )
    order = jnp.sum(ahead.astype(jnp.int32), axis=1)
    place = order % head_count * local_pairs + order // head_count
    hit = place[None, :] == pairs[:, None]
    table = jnp.sum(jnp.where(hit, pairs[None, :], 0), axis=1)
    return table, jnp.where(order >= 3 * head_count, most, 0)


def on_device(query_rows, key_rows, value_rows, block_lists, block_counts):
    head_count = lax.axis_size("head")
    seq_count = lax.axis_size("seq")
    part_count = lax.axis_size("parts")
    local_pairs = HEADS // 2 // head_count
    ranks = jnp.stack([lax.axis_index("seq"), lax.axis_index("head")]).astype(jnp.int32)
    table, light_most = place_pairs(block_counts, head_count, local_pairs)
    places = jnp.concatenate([ranks, table])
    groups = [[0], list(range(2, local_pairs)), [1]]
    groups = [group for group in groups if group and group[-1] < local_pairs]

    sources, query_from = [], {}
    for number, group in enumerate(groups):
        parts = [(array, pair) for pair in group for array in (key_rows, value_rows)]
        if len(groups) == 1 or number == 1:
            asked = [0]
        elif number == 0:
            asked = []
        else:
            asked = [1, 2]
        for other in asked:
            query_from[other] = (number, len(parts) * 2)
            parts += [(query_rows, pair) for pair in groups[other]]
        sources.append(gather_columns(places, parts, head_count, local_pairs))

    def spread(source):
        return [source[0]] + [shifted(source[step], "head", step) for step in range(1, head_count)]

    def returned(outs):
        return [outs[0]] + [
            shifted(outs[backward(step, head_count)], "head", step) for step in range(1, head_count)
        ]

    def passed_on(picked):
        return [turned(picked[step - 1], "seq", step) for step in range(1, seq_count)]

    pieces = [spread(sources[0])]
    lists, counts = after((block_lists, block_counts), sources[0])
    lists, counts = lists.reshape(-1), counts.reshape(-1)
    wanted = [turned(lists, "seq", seq_count - step) for step in range(1, seq_count)]

    def pick(number, arrived, light):
        caps = [light if pair >= 3 else PAIR_MOST for pair in groups[number]]
        return pick_blocks(places, counts, wanted, arrived, groups[number][0], caps)

    def whole(number, tile_pairs, blocks, width, into=None):
        source, at = query_from[number]
        group = groups[number]
        return attend(
            places,
            counts,
            tile_pairs,
            pieces[source],
            at,
            blocks,
            group[0],
            len(group),
            width,
            into,
        )

    if len(groups) == 1:
        tile_pairs, picked = pick(0, pieces[0], PAIR_MOST)
        return lay_out(places, [returned(whole(0, tile_pairs, passed_on(picked), 1))], groups)

    pieces.append(spread(after(sources[1], pieces[0], wanted, counts)))
    tile_pairs, picked = pick(0, pieces[0], PAIR_MOST)
    blocks = passed_on(picked)
    light_most = after(jnp.max(after(light_most, sources[0])), pieces[1][1:-1])
    for step in range(1, part_count):
        light_most = jnp.maximum(light_most, turned(light_most[None], "parts", step)[0])
    first = (tile_pairs, blocks)
    ready = pick(1, pieces[1], LIGHT_MOST)
    light_most, first, arrived, ready, third = lax.optimization_barrier(
        (light_most, first, pieces[1], ready, sources[2])
    )

    def finish(light, first, arrived, ready, third):
        pieces[1] = arrived
        tile_pairs, picked = ready if light == LIGHT_MOST else pick(1, arrived, light)
        pieces[2:] = [spread(after(third, picked))]
        second = (tile_pairs, passed_on(picked))
        width = len(groups[0]) + len(groups[1])
        outs = whole(0, *after(first, picked), width)
        arrived = after(pieces[2], outs, second[1])
        tile_pairs, picked = pick(2, arrived, light)
        blocks = passed_on(picked)
        into = (outs, len(groups[0]))
        outs = whole(1, *after(second, picked), width, into)
        results = [returned(outs)]
        source, at = query_from[2]
        state = attend_own(tile_pairs, pieces[source], at, 1)
        outs = attend_far(places, counts, state, pieces[source], at, blocks, groups[2][0], 1)
        results.append(returned(outs))
        return lay_out(places, results, [groups[0] + groups[1], groups[2]])

    if max(max(group) for group in groups) < 3:
        return finish(PAIR_MOST, first, arrived, ready, third)
    return lax.cond(
        light_most > LIGHT_MOST,
        functools.partial(finish, PAIR_MOST),
        functools.partial(finish, LIGHT_MOST),
        first,
        arrived,
        ready,
        third,
    )


def solution(mesh):
    in_specs = (
        P(("parts", "seq", "head"), None),
        P(("parts", "seq", "head"), None),
        P(("parts", "seq", "head"), None),
        P("parts", "seq", None, None),
        P("parts", None, None),
    )
    out_specs = P(("parts", "seq", "head"), None)
    return jax.shard_map(
        on_device, mesh=mesh, in_specs=in_specs, out_specs=out_specs, check_vma=False
    )
```

```python
import functools
import math

import jax
import jax.numpy as jnp
from jax import lax
from jax.experimental import pallas as pl
from jax.experimental.pallas import tpu as pltpu
from jax.sharding import PartitionSpec as P

HEADS = 32
DH = 128
BLOCK = 128
MOST = 3
PAIR_MOST = 4
TILE = 768
PAIR = 2 * DH
LIGHT_MOST = 1
VMEM_LIMIT = 60 * 1024 * 1024 + 448 * 1024
SMEM = pltpu.SMEM
LONG = pl.CostEstimate(flops=2 * 10**11, bytes_accessed=2 * 10**9, transcendentals=0)
BRIEF = pl.CostEstimate(flops=1024, bytes_accessed=1024, transcendentals=0)


def paired(size):
    return size & (size - 1) == 0


def ahead(rank, step, size):
    return rank ^ step if paired(size) else (rank + step) % size


def behind(rank, step, size):
    return rank ^ step if paired(size) else (rank + size - step) % size


def backward(step, size):
    return step if paired(size) else size - step


def shifted(array, axis, step):
    size = lax.axis_size(axis)
    return lax.ppermute(array, axis, [(i, ahead(i, step, size)) for i in range(size)])


def turned(array, axis, step):
    size = lax.axis_size(axis)
    return lax.ppermute(array, axis, [(i, (i + step) % size) for i in range(size)])


def smem_spec():
    return pl.BlockSpec(memory_space=SMEM)


def one_block(shape):
    return pl.BlockSpec(shape, lambda i, *_: (0,) * len(shape))


def gather_kernel(head_count, place_ref, *refs):
    part_count = len(refs) // head_count - 1
    for step in range(head_count):
        for at in range(part_count):
            refs[head_count * part_count + step][:, at * PAIR : (at + 1) * PAIR] = refs[
                step * part_count + at
            ][...]


def gather_columns(places, parts, head_count, local_pairs):
    rows = parts[0][0].shape[0]

    def column_of(step, pair):
        def index(i, place_ref):
            rank = ahead(place_ref[1], step, head_count)
            return 0, place_ref[2 + rank * local_pairs + pair]

        return index

    return pl.pallas_call(
        functools.partial(gather_kernel, head_count),
        grid_spec=pltpu.PrefetchScalarGridSpec(
            num_scalar_prefetch=1,
            grid=(1,),
            in_specs=[
                pl.BlockSpec((rows, PAIR), column_of(step, pair))
                for step in range(head_count)
                for _, pair in parts
            ],
            out_specs=[one_block((rows, len(parts) * PAIR))] * head_count,
        ),
        out_shape=[jax.ShapeDtypeStruct((rows, len(parts) * PAIR), jnp.bfloat16)] * head_count,
        compiler_params=pltpu.CompilerParams(vmem_limit_bytes=VMEM_LIMIT),
        cost_estimate=BRIEF,
        name="gather_columns",
    )(places, *[array for array, _ in parts] * head_count)


def pick_kernel(head_count, seq_count, first_pair, caps, place_ref, counts_ref, *refs):
    want_refs = refs[: seq_count - 1]
    rows_refs = refs[seq_count - 1 : seq_count - 1 + head_count]
    tile_ref = refs[seq_count - 1 + head_count]
    send_refs = refs[seq_count + head_count :]
    my_seq, my_head = place_ref[0], place_ref[1]
    rows = TILE // head_count
    pair_at = 2 + my_head * (HEADS // 2 // head_count) + first_pair
    for step in range(head_count):
        rank = behind(my_head, step, head_count)
        place = pl.ds(pl.multiple_of(rank * rows, 16), rows)
        for pair in range(len(caps)):
            for half in range(2):
                base = pair * 2 * PAIR + half * DH
                tile_ref[2 * pair + half, place, :DH] = rows_refs[step][:, base : base + DH]
                tile_ref[2 * pair + half, place, DH:] = rows_refs[step][
                    :, base + PAIR : base + PAIR + DH
                ]
    for step in range(1, seq_count):
        asker = lax.rem(my_seq + step, seq_count)
        for pair, cap in enumerate(caps):
            first = 2 * place_ref[pair_at + pair]
            first_count = counts_ref[(first * seq_count + asker) * seq_count + my_seq]
            both = first_count + counts_ref[((first + 1) * seq_count + asker) * seq_count + my_seq]
            for slot in range(cap):

                @pl.when(slot < both)
                def _():
                    half = jnp.where(slot < first_count, 0, 1)
                    entry = jnp.where(slot < first_count, slot, slot - first_count)
                    entry = jnp.clip(entry, 0, MOST - 1)
                    block = want_refs[step - 1][
                        ((first + half) * seq_count + my_seq) * MOST + entry
                    ]
                    send_refs[step - 1][pair * PAIR_MOST + slot] = tile_ref[
                        2 * pair + half, pl.ds(pl.multiple_of(block * BLOCK, BLOCK), BLOCK), :
                    ]


def pick_blocks(places, counts, wanted, pieces, first_pair, caps):
    slots = len(caps)
    head_count, seq_count = len(pieces), len(wanted) + 1
    out_shape = [jax.ShapeDtypeStruct((2 * slots, TILE, 2 * DH), jnp.bfloat16)]
    out_shape += [
        jax.ShapeDtypeStruct((sum(caps), BLOCK, 2 * DH), jnp.bfloat16)
    ] * (seq_count - 1)
    outs = pl.pallas_call(
        functools.partial(pick_kernel, head_count, seq_count, first_pair, caps),
        out_shape=out_shape,
        grid=(1,),
        in_specs=[smem_spec()] * (seq_count + 1) + [one_block((pieces[0].shape[0], slots * 2 * PAIR))]
        * head_count,
        out_specs=[one_block(shape.shape) for shape in out_shape],
        compiler_params=pltpu.CompilerParams(vmem_limit_bytes=VMEM_LIMIT),
        cost_estimate=BRIEF,
        name="pick_blocks",
    )(places, counts, *wanted, *pieces)
    return outs[0], outs[1:]


GROUP = 3 * BLOCK


def fold(values, combine):
    total = values[:, :DH]
    for start in range(DH, values.shape[1], DH):
        total = combine(total, values[:, start : start + DH])
    return total


def row_top(scores):
    top = jnp.max(fold(scores, jnp.maximum), axis=1, keepdims=True)
    return jnp.broadcast_to(top, (scores.shape[0], DH))


def weigh(scores, top):
    return jnp.concatenate(
        [jnp.exp2(scores[:, at : at + DH] - top) for at in range(0, scores.shape[1], DH)], axis=1
    )


def start_state(queries, tile_ref, top_ref, sum_ref, mix_ref):
    for start in range(0, TILE, GROUP):
        scores = score(queries, tile_ref[0, start : start + GROUP, :DH], SCALE)
        values = tile_ref[0, start : start + GROUP, DH:]
        add_group(scores, values, top_ref, sum_ref, mix_ref, start == 0)


def add_group(scores, values, top_ref, sum_ref, mix_ref, first):
    top = row_top(scores)
    if not first:
        old_top = top_ref[...]
        top = jnp.maximum(old_top, top)
    weights = weigh(scores, top)
    sums = fold(weights, jnp.add)
    mixture = jnp.dot(weights.astype(jnp.bfloat16), values, preferred_element_type=jnp.float32)
    if not first:
        rescale = jnp.exp2(old_top - top)
        sums = sum_ref[...] * rescale + sums
        mixture = mix_ref[...] * rescale + mixture
    top_ref[...] = top
    sum_ref[...] = sums
    mix_ref[...] = mixture


def score(queries, keys, scale):
    products = lax.dot_general(
        queries, keys, (((1,), (1,)), ((), ())), preferred_element_type=jnp.float32
    )
    return products * scale


SCALE = math.log2(math.e) / math.sqrt(DH)


def block_copies(place_ref, counts_ref, block_refs, kv_ref, sems, head_count, first_pair, turn):
    seq_count = len(block_refs) + 1
    my_seq = place_ref[0]
    half = lax.rem(turn, 2)
    pair_at = 2 + place_ref[1] * (HEADS // 2 // head_count) + first_pair
    first = 2 * place_ref[pair_at + turn // 2]
    slot_most = block_refs[0].shape[0] - 1
    used = jnp.int32(0)
    copies = []
    for step in range(1, seq_count):
        holder = lax.rem(my_seq - step + seq_count, seq_count)
        first_count = counts_ref[(first * seq_count + my_seq) * seq_count + holder]
        second_count = counts_ref[((first + 1) * seq_count + my_seq) * seq_count + holder]
        count = jnp.where(half == 0, first_count, second_count)
        start = jnp.where(half == 0, 0, first_count) + turn // 2 * PAIR_MOST
        for entry in range(MOST):
            place = pl.ds(pl.multiple_of((used + entry) * BLOCK, BLOCK), BLOCK)
            copy = pltpu.make_async_copy(
                block_refs[step - 1].at[jnp.minimum(start + entry, slot_most)],
                kv_ref.at[half, place],
                sems.at[half, len(copies)],
            )
            copies.append((entry < count, copy))
        used = used + count
    return copies, used


def start_copies(copies, also=True):
    for needed, copy in copies:
        pl.when(needed & also)(copy.start)


def wait_copies(copies):
    for needed, copy in copies:
        pl.when(needed)(copy.wait)


def fetch_blocks(place_ref, counts_ref, block_refs, kv_ref, sems, head_count, first_pair):
    turn, turns = pl.program_id(0), pl.num_programs(0)
    shared = (place_ref, counts_ref, block_refs, kv_ref, sems, head_count, first_pair)
    copies, used = block_copies(*shared, turn)

    @pl.when(turn == 0)
    def _():
        kv_ref[...] = jnp.zeros_like(kv_ref)
        start_copies(copies)

    later, _ = block_copies(*shared, jnp.minimum(turn + 1, turns - 1))
    start_copies(later, turn + 1 < turns)
    return copies, used


def visit_blocks(used, q_ref, kv_ref, top_ref, sum_ref, mix_ref):
    half = lax.rem(pl.program_id(0), 2)

    def visit(group, carry):
        place = pl.ds(pl.multiple_of(group * GROUP, GROUP), GROUP)
        column = lax.broadcasted_iota(jnp.int32, (1, GROUP), 1) + group * GROUP
        bias = jnp.where(column < used * BLOCK, 0.0, -jnp.inf)
        scores = score(q_ref[...], kv_ref[half, place, :DH], SCALE) + bias
        add_group(scores, kv_ref[half, place, DH:], top_ref, sum_ref, mix_ref, False)
        return carry

    lax.fori_loop(0, (used + 2) // 3, visit, 0)


def join_pieces(query_refs, q_ref):
    rows = TILE // len(query_refs)
    for step, ref in enumerate(query_refs):
        q_ref[step * rows : (step + 1) * rows, :] = ref[...]


def split_result(out_refs, sum_ref, mix_ref):
    rows = TILE // len(out_refs)
    for step, ref in enumerate(out_refs):
        span = slice(step * rows, (step + 1) * rows)
        total = jnp.sum(sum_ref[span, :], axis=1, keepdims=True)
        ref[...] = (mix_ref[span, :] / total).astype(jnp.bfloat16)


def attend_kernel(head_count, seq_count, first_pair, joined, place_ref, counts_ref, tile_ref, *refs):
    query_refs, refs = refs[:head_count], refs[head_count:]
    block_refs, refs = refs[: seq_count - 1], refs[seq_count - 1 :]
    refs = refs[head_count:] if joined else refs
    out_refs, refs = refs[:head_count], refs[head_count:]
    q_ref, kv_ref, top_ref, sum_ref, mix_ref, sems = refs
    join_pieces(query_refs, q_ref)
    copies, used = fetch_blocks(
        place_ref, counts_ref, block_refs, kv_ref, sems, head_count, first_pair
    )
    start_state(q_ref[...], tile_ref, top_ref, sum_ref, mix_ref)
    wait_copies(copies)
    visit_blocks(used, q_ref, kv_ref, top_ref, sum_ref, mix_ref)
    split_result(out_refs, sum_ref, mix_ref)


def own_kernel(head_count, tile_ref, *refs):
    query_refs, (top_ref, sum_ref, mix_ref, q_ref) = refs[:head_count], refs[head_count:]
    join_pieces(query_refs, q_ref)
    start_state(q_ref[...], tile_ref, top_ref.at[0], sum_ref.at[0], mix_ref.at[0])


def far_kernel(head_count, seq_count, first_pair, place_ref, counts_ref, *refs):
    old_top_ref, old_sum_ref, old_mix_ref = refs[:3]
    query_refs, refs = refs[3 : 3 + head_count], refs[3 + head_count :]
    block_refs, refs = refs[: seq_count - 1], refs[seq_count - 1 :]
    out_refs, refs = refs[:head_count], refs[head_count:]
    q_ref, kv_ref, top_ref, sum_ref, mix_ref, sems = refs
    join_pieces(query_refs, q_ref)
    copies, used = fetch_blocks(
        place_ref, counts_ref, block_refs, kv_ref, sems, head_count, first_pair
    )
    top_ref[...], sum_ref[...], mix_ref[...] = old_top_ref[0], old_sum_ref[0], old_mix_ref[0]
    wait_copies(copies)
    visit_blocks(used, q_ref, kv_ref, top_ref, sum_ref, mix_ref)
    split_result(out_refs, sum_ref, mix_ref)


def state_spec():
    return pl.BlockSpec((1, TILE, DH), lambda i: (i, 0, 0))


def tile_spec():
    return pl.BlockSpec((1, TILE, 2 * DH), lambda i: (i, 0, 0))


def query_specs(queries, query_at):
    return [pl.BlockSpec((piece.shape[0], DH), lambda i: (0, query_at + i)) for piece in queries]


def attention_call(kernel, name, slots, seq_count, operands, in_specs, head_count, width, into):
    written = into[1] if into else 0
    operands = list(operands) + list(into[0] if into else [])
    aliases = {len(operands) - head_count + i: i for i in range(head_count)} if into else {}
    in_specs = in_specs + ([pl.BlockSpec(memory_space=pltpu.HBM)] * head_count if into else [])
    most_blocks = -(-(seq_count - 1) * MOST // 3) * 3
    rows = TILE // head_count
    return pl.pallas_call(
        kernel,
        grid=(2 * slots,),
        out_shape=[jax.ShapeDtypeStruct((rows, width * PAIR), jnp.bfloat16)] * head_count,
        in_specs=in_specs,
        out_specs=[pl.BlockSpec((rows, DH), lambda i: (0, 2 * written + i))] * head_count,
        scratch_shapes=[
            pltpu.VMEM((TILE, DH), jnp.bfloat16),
            pltpu.VMEM((2, most_blocks * BLOCK, 2 * DH), jnp.bfloat16),
            pltpu.VMEM((TILE, DH), jnp.float32),
            pltpu.VMEM((TILE, DH), jnp.float32),
            pltpu.VMEM((TILE, DH), jnp.float32),
            pltpu.SemaphoreType.DMA((2, MOST * (seq_count - 1))),
        ],
        input_output_aliases=aliases,
        compiler_params=pltpu.CompilerParams(vmem_limit_bytes=VMEM_LIMIT),
        cost_estimate=LONG if name == "attend_far" else BRIEF,
        name=name,
    )(*operands)


def attend(
    places, counts, tile_pairs, queries, query_at, blocks, first_pair, slots, width, into=None
):
    head_count, seq_count = len(queries), len(blocks) + 1
    return attention_call(
        functools.partial(attend_kernel, head_count, seq_count, first_pair, bool(into)),
        "attend",
        slots,
        seq_count,
        (places, counts, tile_pairs, *queries, *blocks),
        [smem_spec()] * 2
        + [tile_spec()]
        + query_specs(queries, query_at)
        + [pl.BlockSpec(memory_space=pl.ANY)] * len(blocks),
        head_count,
        width,
        into,
    )


def attend_own(tile_pairs, queries, query_at, slots):
    head_count = len(queries)
    return pl.pallas_call(
        functools.partial(own_kernel, head_count),
        grid=(2 * slots,),
        out_shape=[jax.ShapeDtypeStruct((2 * slots, TILE, DH), jnp.float32)] * 3,
        in_specs=[tile_spec()] + query_specs(queries, query_at),
        out_specs=[state_spec()] * 3,
        scratch_shapes=[pltpu.VMEM((TILE, DH), jnp.bfloat16)],
        compiler_params=pltpu.CompilerParams(vmem_limit_bytes=VMEM_LIMIT),
        cost_estimate=BRIEF,
        name="attend_own",
    )(tile_pairs, *queries)


def attend_far(places, counts, state, queries, query_at, blocks, first_pair, slots):
    head_count, seq_count = len(queries), len(blocks) + 1
    return attention_call(
        functools.partial(far_kernel, head_count, seq_count, first_pair),
        "attend_far",
        slots,
        seq_count,
        (places, counts, *state, *queries, *blocks),
        [smem_spec()] * 2
        + [state_spec()] * 3
        + query_specs(queries, query_at)
        + [pl.BlockSpec(memory_space=pl.ANY)] * len(blocks),
        head_count,
        slots,
        None,
    )


def lay_kernel(groups, head_count, place_ref, *refs):
    out_ref = refs[-1]
    local_pairs = HEADS // 2 // head_count
    for number, group in enumerate(groups):
        for step in range(head_count):
            rank = behind(place_ref[1], step, head_count)
            for at, pair in enumerate(group):
                column = place_ref[2 + rank * local_pairs + pair] * PAIR
                out_ref[:, pl.ds(pl.multiple_of(column, PAIR), PAIR)] = refs[
                    number * head_count + step
                ][:, at * PAIR : (at + 1) * PAIR]


def lay_out(places, stages, groups):
    head_count = len(stages[0])
    rows = stages[0][0].shape[0]
    flat = [piece for stage in stages for piece in stage]
    return pl.pallas_call(
        functools.partial(lay_kernel, groups, head_count),
        grid=(1,),
        out_shape=jax.ShapeDtypeStruct((rows, HEADS * DH), jnp.bfloat16),
        in_specs=[smem_spec()] + [one_block(piece.shape) for piece in flat],
        out_specs=one_block((rows, HEADS * DH)),
        compiler_params=pltpu.CompilerParams(vmem_limit_bytes=VMEM_LIMIT),
        cost_estimate=BRIEF,
        name="lay_out",
    )(places, *flat)


def after(value, *others):
    return lax.optimization_barrier((value, others))[0]


def place_pairs(block_counts, head_count, local_pairs):
    pair_count = HEADS // 2
    listed = jnp.sum(block_counts.reshape(pair_count, 2, *block_counts.shape[1:]), axis=1)
    total = jnp.sum(listed, axis=(1, 2))
    most = jnp.max(listed, axis=(1, 2))
    pairs = jnp.arange(pair_count, dtype=jnp.int32)
    ahead = (total[None, :] > total[:, None]) | (
        (total[None, :] == total[:, None]) & (pairs[None, :] < pairs[:, None])
    )
    order = jnp.sum(ahead.astype(jnp.int32), axis=1)
    place = order % head_count * local_pairs + order // head_count
    hit = place[None, :] == pairs[:, None]
    table = jnp.sum(jnp.where(hit, pairs[None, :], 0), axis=1)
    return table, jnp.where(order >= 3 * head_count, most, 0)


def on_device(query_rows, key_rows, value_rows, block_lists, block_counts):
    head_count = lax.axis_size("head")
    seq_count = lax.axis_size("seq")
    part_count = lax.axis_size("parts")
    local_pairs = HEADS // 2 // head_count
    ranks = jnp.stack([lax.axis_index("seq"), lax.axis_index("head")]).astype(jnp.int32)
    table, light_most = place_pairs(block_counts, head_count, local_pairs)
    places = jnp.concatenate([ranks, table])
    groups = [[0], list(range(2, local_pairs)), [1]]
    groups = [group for group in groups if group and group[-1] < local_pairs]

    sources, query_from = [], {}
    for number, group in enumerate(groups):
        parts = [(array, pair) for pair in group for array in (key_rows, value_rows)]
        if len(groups) == 1 or number == 1:
            asked = [0]
        elif number == 0:
            asked = []
        else:
            asked = [1, 2]
        for other in asked:
            query_from[other] = (number, len(parts) * 2)
            parts += [(query_rows, pair) for pair in groups[other]]
        sources.append(gather_columns(places, parts, head_count, local_pairs))

    def spread(source):
        return [source[0]] + [shifted(source[step], "head", step) for step in range(1, head_count)]

    def returned(outs):
        return [outs[0]] + [
            shifted(outs[backward(step, head_count)], "head", step) for step in range(1, head_count)
        ]

    def passed_on(picked):
        return [turned(picked[step - 1], "seq", step) for step in range(1, seq_count)]

    pieces = [spread(sources[0])]
    lists, counts = after((block_lists, block_counts), sources[0])
    lists, counts = lists.reshape(-1), counts.reshape(-1)
    wanted = [turned(lists, "seq", seq_count - step) for step in range(1, seq_count)]

    def pick(number, arrived, light):
        caps = [light if pair >= 3 else PAIR_MOST for pair in groups[number]]
        return pick_blocks(places, counts, wanted, arrived, groups[number][0], caps)

    def whole(number, tile_pairs, blocks, width, into=None):
        source, at = query_from[number]
        group = groups[number]
        return attend(
            places,
            counts,
            tile_pairs,
            pieces[source],
            at,
            blocks,
            group[0],
            len(group),
            width,
            into,
        )

    if len(groups) == 1:
        tile_pairs, picked = pick(0, pieces[0], PAIR_MOST)
        return lay_out(places, [returned(whole(0, tile_pairs, passed_on(picked), 1))], groups)

    pieces.append(spread(after(sources[1], pieces[0], wanted, counts)))
    tile_pairs, picked = pick(0, pieces[0], PAIR_MOST)
    blocks = passed_on(picked)
    light_most = after(jnp.max(after(light_most, sources[0])), pieces[1][1:-1])
    for step in range(1, part_count):
        light_most = jnp.maximum(light_most, turned(light_most[None], "parts", step)[0])
    first = (tile_pairs, blocks)
    ready = pick(1, pieces[1], LIGHT_MOST)
    light_most, first, arrived, ready, third = lax.optimization_barrier(
        (light_most, first, pieces[1], ready, sources[2])
    )

    def finish(light, first, arrived, ready, third):
        pieces[1] = arrived
        tile_pairs, picked = ready if light == LIGHT_MOST else pick(1, arrived, light)
        pieces[2:] = [spread(after(third, picked))]
        second = (tile_pairs, passed_on(picked))
        width = len(groups[0]) + len(groups[1])
        outs = whole(0, *after(first, picked), width)
        arrived = after(pieces[2], outs, second[1])
        tile_pairs, picked = pick(2, arrived, light)
        blocks = passed_on(picked)
        into = (outs, len(groups[0]))
        outs = whole(1, *after(second, picked), width, into)
        results = [returned(outs)]
        source, at = query_from[2]
        state = attend_own(tile_pairs, pieces[source], at, 1)
        outs = attend_far(places, counts, state, pieces[source], at, blocks, groups[2][0], 1)
        results.append(returned(outs))
        return lay_out(places, results, [groups[0] + groups[1], groups[2]])

    if max(max(group) for group in groups) < 3:
        return finish(PAIR_MOST, first, arrived, ready, third)
    return lax.cond(
        light_most > LIGHT_MOST,
        functools.partial(finish, PAIR_MOST),
        functools.partial(finish, LIGHT_MOST),
        first,
        arrived,
        ready,
        third,
    )


def solution(mesh):
    in_specs = (
        P(("parts", "seq", "head"), None),
        P(("parts", "seq", "head"), None),
        P(("parts", "seq", "head"), None),
        P("parts", "seq", None, None),
        P("parts", None, None),
    )
    out_specs = P(("parts", "seq", "head"), None)
    return jax.shard_map(
        on_device, mesh=mesh, in_specs=in_specs, out_specs=out_specs, check_vma=False
    )
```
